128 devices in a mesh: fine: 128 (over z, x, y, core).
Axes of the slice: x: 4, y: 4, z: 4, core: 2. Of those that a mesh axis runs over, the one named last changes fastest.
Arguments:
- right_side: float32 [8192, 4, 64], P('fine'), may hold values from -8 to 8
- fine_vals: float32 [8192, 7, 4096], P('fine'), as said below
- fine_cols: int32 [8192, 6], P('fine'), may hold values from 0 to 8191, as said below
- prol_vals: float32 [8192, 4096], P('fine'), may hold values from -0.25 to 0.25
- prol_cols: int32 [8192], P('fine'), may hold values from 0 to 1023, as said below
- coarse_vals: float32 [1024, 7, 4096], P('fine'), as said below
- coarse_cols: int32 [1024, 6], P('fine'), may hold values from 0 to 1023, as said below
Outputs:
- solution: float32 [8192, 4, 64], P('fine')
- residual: float32 [8192, 4, 64], P('fine')
The draws below stay inside these ranges and needn't reach their ends.
Inputs may be any that keep to these rules, and one draw needn't show every extreme that they name: `fine_cols`: row i's block columns lie on the device that holds block i or on the one before or after it, counted cyclically, 64 blocks a device. `prol_cols`: fine block i's coarse block is i // 8 or one of the two next to it, counted cyclically. `coarse_cols`: row c's block columns lie on the device that holds coarse block c or on the one before or after it, counted cyclically, 8 coarse blocks a device. `fine_vals`: slot 0 multiplies the row's own block. `coarse_vals`: slot 0 multiplies the row's own block.
All inputs are finite; a program needn't handle non-finite values.
Results may differ from the reference program's by a relative error of at most 0.0015.
Values sent between devices are 32-bit elements; how exact they have to be, the bound alone decides.
No kernel may reach another device: no remote copies, remote signals or barrier semaphores. Data moves between devices by JAX's collectives and lax.ppermute only.
A program may use at most 128 MiB of HBM per device.

```python
import jax
import jax.numpy as jnp
from jax import lax

NB_DEV = 64
B = 64
F = 4
K = 7
KC = 7
NBLK = 8192
NC = 1024


def operator_blocks(key, rows, slots):
    noise = 0.025 * jax.random.normal(key, (rows, slots, B, B), jnp.float32)
    first = (jnp.arange(slots) == 0).astype(jnp.float32)[:, None, None]
    blocks = noise + first * jnp.eye(B, dtype=jnp.float32)[None]
    return blocks.reshape(rows, slots, B * B)


def near_columns(key, rows, slots, per_device, total):
    offset = jax.random.randint(key, (rows, slots), 0, 3 * per_device)
    owner = jnp.arange(rows, dtype=jnp.int32) // per_device
    start = (owner - 1) * per_device
    return jnp.mod(start[:, None] + offset, total).astype(jnp.int32)


def draw_fine_vals(key, part):
    key = jax.random.fold_in(key, 11)
    return operator_blocks(key, NBLK, K)


def draw_coarse_vals(key, part):
    key = jax.random.fold_in(key, 23)
    return operator_blocks(key, NC, KC)


def draw_fine_cols(key, part):
    key = jax.random.fold_in(key, 37)
    return near_columns(key, NBLK, K - 1, NB_DEV, NBLK)


def draw_coarse_cols(key, part):
    key = jax.random.fold_in(key, 53)
    return near_columns(key, NC, KC - 1, NB_DEV // 8, NC)


def draw_prol_cols(key, part):
    key = jax.random.fold_in(key, 41)
    pick = jax.random.randint(key, (NBLK,), 0, 8)
    step = jnp.where(pick == 0, -1, jnp.where(pick == 1, 1, 0)).astype(jnp.int32)
    base = jnp.arange(NBLK, dtype=jnp.int32) // 8
    return jnp.mod(base + step, NC).astype(jnp.int32)


def levels(rng, dims, pieces, smallest, top_value):
    def one(position, blocks):
        steps = jax.random.uniform(jax.random.fold_in(jax.random.fold_in(rng, 6), position), (blocks,), jnp.float32, smallest / len(pieces), top_value / len(pieces))
        return jnp.repeat(jnp.exp(steps), dims[position] // blocks).reshape((-1,) + (1,) * (len(dims) - position - 1))

    loudness = one(*pieces[0])
    for cut in pieces[1:]:
        loudness = loudness * one(*cut)
    return loudness


def gaussian(key, extent, scale, most, split=(), held_as=jnp.bfloat16):
    level = levels(key, extent, split, -0.22, 0.18) if split else 1.0
    entries = jax.random.normal(key, extent, jnp.float32) * scale * level
    return jnp.minimum(jnp.maximum(entries, -most), most).astype(held_as)


def setup_inputs(seed: int = 0) -> dict:
    streams_of = jax.random.split(jax.random.key(seed), 8)
    right_side = gaussian(streams_of[0], (NBLK, F, B), 1.0, 8.0, ((0, 128),), jnp.float32)
    fine_vals = draw_fine_vals(jax.random.fold_in(streams_of[7], 71), 0)
    fine_cols = draw_fine_cols(jax.random.fold_in(streams_of[7], 71), 0)
    prol_vals = gaussian(streams_of[3], (NBLK, B * B), (8 * B) ** -0.5, 0.25, ((0, 128),), jnp.float32)
    prol_cols = draw_prol_cols(jax.random.fold_in(streams_of[7], 71), 0)
    coarse_vals = draw_coarse_vals(jax.random.fold_in(streams_of[7], 71), 0)
    coarse_cols = draw_coarse_cols(jax.random.fold_in(streams_of[7], 71), 0)
    return {"right_side": right_side, "fine_vals": fine_vals, "fine_cols": fine_cols, "prol_vals": prol_vals, "prol_cols": prol_cols, "coarse_vals": coarse_vals, "coarse_cols": coarse_cols}


THETA = 1.0
DELTA = 0.75
SIGMA = THETA / DELTA


def apply_blocks(vector, vals, cols):
    own = jnp.einsum('bij,bfj->bfi', vals[:, 0], vector, precision=lax.Precision.HIGHEST)
    near = vector[cols]
    other = jnp.einsum('bkij,bkfj->bfi', vals[:, 1:], near, precision=lax.Precision.HIGHEST)
    return own + other


def smooth(resid, operate):
    d = resid / THETA
    x = d
    rho = 1.0 / SIGMA
    for step in range(2):
        resid = resid - operate(d)
        rho_new = 1.0 / (2.0 * SIGMA - rho)
        d = rho_new * rho * d + (2.0 * rho_new / DELTA) * resid
        x = x + d
        rho = rho_new
    return x


def reference(right_side, fine_vals, fine_cols, prol_vals, prol_cols, coarse_vals, coarse_cols):
    fine_blocks = fine_vals.reshape(NBLK, K, B, B)
    prol_blocks = prol_vals.reshape(NBLK, B, B)
    coarse_blocks = coarse_vals.reshape(NC, KC, B, B)

    def fine_op(v):
        return apply_blocks(v, fine_blocks, fine_cols)

    def coarse_op(v):
        return apply_blocks(v, coarse_blocks, coarse_cols)

    def cycle(resid):
        x = smooth(resid, fine_op)
        second = resid - fine_op(x)
        terms = jnp.einsum('bji,bfj->bfi', prol_blocks, second, precision=lax.Precision.HIGHEST)
        restricted = jax.ops.segment_sum(terms, prol_cols, num_segments=NC)
        coarse_fix = smooth(restricted, coarse_op)
        x = x + jnp.einsum('bij,bfj->bfi', prol_blocks, coarse_fix[prol_cols], precision=lax.Precision.HIGHEST)
        third = resid - fine_op(x)
        return x + smooth(third, fine_op)

    first = cycle(right_side)
    solution = first + cycle(right_side - fine_op(first))
    return solution, right_side - fine_op(solution)
```

```python
import functools

import jax
import jax.numpy as jnp
from jax import lax
from jax.experimental import pallas as pl
from jax.experimental.pallas import tpu as pltpu
from jax.sharding import PartitionSpec as P

THETA = 1.0
DELTA = 0.75
SIGMA = THETA / DELTA
RHO0 = 1.0 / SIGMA
RHO1 = 1.0 / (2.0 * SIGMA - RHO0)
RHO2 = 1.0 / (2.0 * SIGMA - RHO1)
STEP1 = (RHO1 * RHO0, 2.0 * RHO1 / DELTA)
STEP2 = (RHO2 * RHO1, 2.0 * RHO2 / DELTA)

F32 = jnp.float32
BF16 = jnp.bfloat16
VMEM = pl.BlockSpec(memory_space=pltpu.VMEM)
SMEM = pl.BlockSpec(memory_space=pltpu.SMEM)
PARAMS = pltpu.CompilerParams(vmem_limit_bytes=24 * 2**20)


def same_half():
    row = lax.broadcasted_iota(jnp.int32, (1, 8, 128), 1)
    lane = lax.broadcasted_iota(jnp.int32, (1, 8, 128), 2)
    return (row % 2) == (lane // 64)


def even_row():
    return (lax.broadcasted_iota(jnp.int32, (1, 8, 128), 1) % 2) == 0


def other_row(x):
    return jnp.where(even_row(), pltpu.roll(x, 7, 1), pltpu.roll(x, 1, 1))


def pack_halves(whole):
    half = whole.shape[0] // 2
    return jnp.where(same_half(), whole[:half], whole[half:])


def two_parts(x):
    high = x.astype(BF16).astype(F32)
    return high, x - high


def masked_rows(packed):
    mask = same_half()
    first = jnp.where(mask, packed, 0.0)
    second = pltpu.roll(jnp.where(mask, 0.0, packed), 64, 2)
    high, low = two_parts(jnp.concatenate([first, second], 0))
    return jnp.concatenate([high, low], 1).astype(BF16)


def own_lane(width):
    return lax.broadcasted_iota(jnp.int32, (8, width), 1) % 8


def from_pairs(rows):
    n = rows.shape[0]
    pair = lax.broadcasted_iota(jnp.int32, (256, 256), 0) // 8
    lane = lax.broadcasted_iota(jnp.int32, (256, 256), 1)
    spread = ((lane % 64) == 2 * pair + lane // 128).astype(F32).astype(BF16)
    high, low = two_parts(rows.reshape(n * 8, 256))
    both = jnp.concatenate([high, low], 0).astype(BF16)
    y = jnp.dot(both, spread, preferred_element_type=F32)
    y = (y[: n * 8] + y[n * 8 :]).reshape(n, 8, 256)
    y = jnp.where(even_row(), y[:, :, :128], y[:, :, 128:])
    return pack_halves(y + other_row(y))


def row_products(left, high_ref, low_ref, group):
    out = jnp.dot(left, high_ref[group], preferred_element_type=F32)
    return out + jnp.dot(left, low_ref[group], preferred_element_type=F32)


def pick_rows(out):
    picked = []
    lane = own_lane(out.shape[1])
    for r in range(8):
        both = out[16 * r : 16 * r + 8] + out[16 * r + 8 : 16 * r + 16]
        picked.append(jnp.where(lane == r, both, 0.0)[None])
    return picked


def fill_window(window, own, partner, outer):
    n = 2 * own.shape[0]
    window[0:n] = masked_rows(partner[...])
    window[n : 2 * n] = masked_rows(own[...])
    window[2 * n : 3 * n] = masked_rows(outer[...])


def operator(col, slots, window, left, high_ref, low_ref, first):
    picked = []
    for g in range(high_ref.shape[0]):
        for i in range(8 * g, 8 * g + 8):
            for k in range(slots):
                at = first + i if (first is not None and k == 0) else col(i, k)
                left[16 * i : 16 * i + 16, 128 * k : 128 * k + 128] = window[at]
        out = row_products(left[128 * g : 128 * g + 128, 0 : 128 * slots], high_ref, low_ref, g)
        picked += pick_rows(out)
    return from_pairs(jnp.concatenate(picked, 0))


def prepare_kernel(slots, vals, high_ref, low_ref):
    g = pl.program_id(0)
    for k in range(slots):
        block = jnp.concatenate([vals[k, :, 128 * t : 128 * t + 128] for t in range(32)], 0).T
        high, low = two_parts(block)
        high_ref[g, 128 * k : 128 * k + 128, :] = high.astype(BF16)
        low_ref[g, 128 * k : 128 * k + 128, :] = low.astype(BF16)


def prepare(vals):
    rows, slots, width = vals.shape
    shape = jax.ShapeDtypeStruct((rows // 8, 128 * slots, 256), BF16)
    return pl.pallas_call(
        functools.partial(prepare_kernel, slots),
        grid=(rows // 8,),
        in_specs=[pl.BlockSpec((slots, 8, width), lambda g: (0, g, 0))],
        out_specs=[VMEM, VMEM],
        out_shape=[shape, shape],
        compiler_params=PARAMS,
        name="prepare",
    )(vals.transpose(1, 0, 2))


def prepare_transfer_kernel(vals, high_ref, low_ref, high_back_ref, low_back_ref):
    g = pl.program_id(0)
    block = jnp.concatenate([vals[:, 128 * t : 128 * t + 128] for t in range(32)], 0)
    high, low = two_parts(block)
    high_back_ref[g] = high.astype(BF16)
    low_back_ref[g] = low.astype(BF16)
    high, low = two_parts(block.T)
    high_ref[g] = high.astype(BF16)
    low_ref[g] = low.astype(BF16)


def prepare_transfer(vals):
    rows, width = vals.shape
    out = jax.ShapeDtypeStruct((rows // 8, 128, 256), BF16)
    back = jax.ShapeDtypeStruct((rows // 8, 256, 128), BF16)
    return pl.pallas_call(
        prepare_transfer_kernel,
        grid=(rows // 8,),
        in_specs=[pl.BlockSpec((8, width), lambda g: (g, 0))],
        out_specs=[VMEM] * 4,
        out_shape=[out, out, back, back],
        compiler_params=PARAMS,
        name="prepare_transfer",
    )(vals)


def restrict(prol_col, vector, high_ref, low_ref, total, partner_ref, own_ref, outer_ref):
    rows = masked_rows(vector)
    n = rows.shape[0]
    lane = lax.broadcasted_iota(jnp.int32, (128, 256), 0)
    pair = lax.broadcasted_iota(jnp.int32, (128, 256), 1) // 8
    gather = ((lane % 64) == 2 * pair + lane // 64).astype(F32).astype(BF16)
    pairs = jnp.dot(rows.reshape(16 * n, 128), gather, preferred_element_type=F32)
    lane16 = lax.broadcasted_iota(jnp.int32, (16, 256), 1) % 8
    total[...] = jnp.zeros_like(total)
    mask = same_half()[0]
    for g in range(n // 8):
        left = []
        for r in range(8):
            at = 128 * g + 16 * r
            left.append(jnp.where(lane16 == r, pairs[at : at + 16], 0.0))
        out = row_products(jnp.concatenate(left, 0).astype(BF16), high_ref, low_ref, g)
        for r in range(8):
            both = out[16 * r : 16 * r + 8] + out[16 * r + 8 : 16 * r + 16]
            c = prol_col[8 * g + r]
            total[c] = total[c] + jnp.where(mask, both, 0.0)
    whole = total[...]
    whole = whole + pltpu.roll(whole, 64, 2)
    whole = whole + other_row(whole)
    m = whole.shape[0] // 3
    partner_ref[...] = pack_halves(whole[:m])
    own_ref[...] = pack_halves(whole[m : 2 * m])
    outer_ref[...] = pack_halves(whole[2 * m :])


def smooth_kernel(step, count, col, own, partner, outer, high, low, resid, total, new_resid, new_d, new_total, window, left):
    fill_window(window, own, partner, outer)
    product = operator(lambda i, k: col[k - 1, i], 7, window, left, high, low, count)
    r = resid[...] - product
    d = step[0] * own[...] + step[1] * r
    new_resid[...] = r
    new_d[...] = d
    new_total[...] = total[...] + d


def restrict_kernel(
    count, col, prol_col, own, partner, outer, high, low, resid, back_high, back_low,
    new_resid, to_partner, to_own, to_outer, window, left, sums,
):
    fill_window(window, own, partner, outer)
    product = operator(lambda i, k: col[k - 1, i], 7, window, left, high, low, count)
    r = resid[...] - product
    new_resid[...] = r
    restrict(prol_col, r, back_high, back_low, sums, to_partner, to_own, to_outer)


def prolong_kernel(prol_col, own, partner, outer, high, low, total, spread, new_total, window, left):
    fill_window(window, own, partner, outer)
    product = operator(lambda i, k: prol_col[i], 1, window, left, high, low, None)
    spread[...] = product
    new_total[...] = total[...] + product


def resid_kernel(count, col, own, partner, outer, high, low, resid, total, new_resid, new_total, window, left):
    fill_window(window, own, partner, outer)
    product = operator(lambda i, k: col[k - 1, i], 7, window, left, high, low, count)
    r = resid[...] - product
    new_resid[...] = r
    new_total[...] = total[...] + r


def call(kernel, name, scalars, vectors, outs, window_blocks, slots, rows, extra=()):
    return pl.pallas_call(
        kernel,
        in_specs=[SMEM] * len(scalars) + [VMEM] * len(vectors),
        out_specs=[VMEM] * len(outs),
        out_shape=[jax.ShapeDtypeStruct((n // 2, 8, 128), F32) for n in outs],
        scratch_shapes=[
            pltpu.VMEM((window_blocks, 16, 128), BF16),
            pltpu.VMEM((16 * rows, 128 * slots), BF16),
            *extra,
        ],
        compiler_params=PARAMS,
        name=name,
    )(*scalars, *vectors)


def to_packed(vector):
    half = vector.shape[0] // 2
    first, second = vector[:half], vector[half:]
    even = jnp.concatenate([first, second], -1)
    odd = jnp.concatenate([second, first], -1)
    return jnp.stack([even, odd], 2).reshape(half, 8, 128)


def from_packed(packed):
    split = packed.reshape(-1, 4, 2, 2, 64)
    return jnp.concatenate([split[:, :, 0, 0], split[:, :, 0, 1]], 0)


def body(right_side, fine_vals, fine_cols, prol_vals, prol_cols, coarse_vals, coarse_cols):
    devices = lax.axis_size("fine")
    rank = lax.axis_index("fine")
    n = right_side.shape[0]
    m = coarse_vals.shape[0]
    partner_rank = rank ^ 1

    def window_index(cols, per_device):
        owner = cols // per_device
        place = cols - owner * per_device
        slot = jnp.where(owner == rank, 1, jnp.where(owner == partner_rank, 0, 2))
        return (slot * per_device + place).astype(jnp.int32)

    fine_at = window_index(fine_cols.T, n)
    prol_at = window_index(prol_cols, m)
    coarse_at = window_index(coarse_cols.T, m)

    inside = [(i, i ^ 1) for i in range(devices)]
    across = []
    for i in range(1, devices, 2):
        across += [(i, (i + 1) % devices), ((i + 1) % devices, i)]

    def swap(to_partner, to_outer):
        outer = lax.ppermute(to_outer, "fine", across)
        partner = lax.ppermute(to_partner, "fine", inside)
        return partner, outer

    high, low = prepare(fine_vals)
    coarse_high, coarse_low = prepare(coarse_vals)
    prol_high, prol_low, back_high, back_low = prepare_transfer(prol_vals)

    def fine(kernel, name, d, more, outs, scalars=(), extra=(), after=()):
        partner, outer = swap(d, d)
        vectors = (d, partner, outer, high, low, *more, *after)
        return call(kernel, name, (fine_at, *scalars), vectors, outs, 3 * n, 7, n, extra)

    def coarse(d, resid, total, step):
        partner, outer = swap(d, d)
        kernel = functools.partial(smooth_kernel, step, m)
        vectors = (d, partner, outer, coarse_high, coarse_low, resid, total)
        return call(kernel, "coarse_smooth", (coarse_at,), vectors, [m, m, m], 3 * m, 7, m)

    def fine_smooth(d, resid, total, step):
        return fine(functools.partial(smooth_kernel, step, n), "fine_smooth", d, (resid, total), [n, n, n])

    def fine_resid(d, resid, total):
        return fine(functools.partial(resid_kernel, n), "fine_resid", d, (resid, total), [n, n])

    def cycle(resid, total):
        resid, d, total = fine_smooth(resid, resid, total, STEP1)
        resid, d, total = fine_smooth(d, resid, total, STEP2)
        second, to_partner, to_own, to_outer = fine(
            functools.partial(restrict_kernel, n), "fine_restrict", d, (resid,), [n, m, m, m],
            scalars=(prol_at,), extra=(pltpu.VMEM((3 * m, 8, 128), F32),), after=(back_high, back_low),
        )
        partner, outer = swap(to_partner, to_outer)
        right = to_own + partner + outer
        resid, d, fix = coarse(right, right, right, STEP1)
        resid, d, fix = coarse(d, resid, fix, STEP2)
        partner, outer = swap(fix, fix)
        spread, total = call(
            prolong_kernel, "prolong", (prol_at,),
            (fix, partner, outer, prol_high, prol_low, total), [n, n], 3 * m, 1, n,
        )
        resid, total = fine_resid(spread, second, total)
        resid, d, total = fine_smooth(resid, resid, total, STEP1)
        resid, d, total = fine_smooth(d, resid, total, STEP2)
        return d, resid, total

    first = to_packed(right_side)
    d, resid, total = cycle(first, first)
    resid, total = fine_resid(d, resid, total)
    d, resid, total = cycle(resid, total)
    resid, _ = fine_resid(d, resid, total)
    return from_packed(total), from_packed(resid)


def solution(mesh):
    in_specs = (
        P("fine", None, None),
        P("fine", None, None),
        P("fine", None),
        P("fine", None),
        P("fine"),
        P("fine", None, None),
        P("fine", None),
    )
    out_specs = (P("fine", None, None), P("fine", None, None))
    return jax.shard_map(body, mesh=mesh, in_specs=in_specs, out_specs=out_specs, check_vma=False)
```

```python
import functools

import jax
import jax.numpy as jnp
from jax import lax
from jax.experimental import pallas as pl
from jax.experimental.pallas import tpu as pltpu
from jax.sharding import PartitionSpec as P

THETA = 1.0
DELTA = 0.75
SIGMA = THETA / DELTA
RHO0 = 1.0 / SIGMA
RHO1 = 1.0 / (2.0 * SIGMA - RHO0)
RHO2 = 1.0 / (2.0 * SIGMA - RHO1)
STEP1 = (RHO1 * RHO0, 2.0 * RHO1 / DELTA)
STEP2 = (RHO2 * RHO1, 2.0 * RHO2 / DELTA)

F32 = jnp.float32
BF16 = jnp.bfloat16
VMEM = pl.BlockSpec(memory_space=pltpu.VMEM)
SMEM = pl.BlockSpec(memory_space=pltpu.SMEM)
PARAMS = pltpu.CompilerParams(vmem_limit_bytes=16 * 2**20)


def same_half():
    row = lax.broadcasted_iota(jnp.int32, (1, 8, 128), 1)
    lane = lax.broadcasted_iota(jnp.int32, (1, 8, 128), 2)
    return (row % 2) == (lane // 64)


def even_row():
    return (lax.broadcasted_iota(jnp.int32, (1, 8, 128), 1) % 2) == 0


def other_row(x):
    return jnp.where(even_row(), pltpu.roll(x, 7, 1), pltpu.roll(x, 1, 1))


def pack_halves(whole):
    half = whole.shape[0] // 2
    return jnp.where(same_half(), whole[:half], whole[half:])


def two_parts(x):
    high = x.astype(BF16).astype(F32)
    return high, x - high


def masked_rows(packed):
    mask = same_half()
    first = jnp.where(mask, packed, 0.0)
    second = pltpu.roll(jnp.where(mask, 0.0, packed), 64, 2)
    high, low = two_parts(jnp.concatenate([first, second], 0))
    return jnp.concatenate([high, low], 1).astype(BF16)


def own_lane(width):
    return lax.broadcasted_iota(jnp.int32, (8, width), 1) % 8


def from_pairs(rows):
    n = rows.shape[0]
    pair = lax.broadcasted_iota(jnp.int32, (256, 256), 0) // 8
    lane = lax.broadcasted_iota(jnp.int32, (256, 256), 1)
    spread = ((lane % 64) == 2 * pair + lane // 128).astype(F32).astype(BF16)
    high, low = two_parts(rows.reshape(n * 8, 256))
    both = jnp.concatenate([high, low], 0).astype(BF16)
    y = jnp.dot(both, spread, preferred_element_type=F32)
    y = (y[: n * 8] + y[n * 8 :]).reshape(n, 8, 256)
    y = jnp.where(even_row(), y[:, :, :128], y[:, :, 128:])
    return pack_halves(y + other_row(y))


def row_products(left, high_ref, low_ref, group):
    out = jnp.dot(left, high_ref[group], preferred_element_type=F32)
    return out + jnp.dot(left, low_ref[group], preferred_element_type=F32)


def pick_rows(out):
    picked = []
    lane = own_lane(out.shape[1])
    for r in range(8):
        both = out[16 * r : 16 * r + 8] + out[16 * r + 8 : 16 * r + 16]
        picked.append(jnp.where(lane == r, both, 0.0)[None])
    return picked


def fill_window(window, own, partner, outer):
    n = 2 * own.shape[0]
    window[0:n] = masked_rows(partner[...])
    window[n : 2 * n] = masked_rows(own[...])
    window[2 * n : 3 * n] = masked_rows(outer[...])


def operator(col, slots, window, left, high_ref, low_ref, first):
    picked = []
    for g in range(high_ref.shape[0]):
        for i in range(8 * g, 8 * g + 8):
            for k in range(slots):
                at = first + i if (first is not None and k == 0) else col(i, k)
                left[16 * i : 16 * i + 16, 128 * k : 128 * k + 128] = window[at]
        out = row_products(left[128 * g : 128 * g + 128, 0 : 128 * slots], high_ref, low_ref, g)
        picked += pick_rows(out)
    return from_pairs(jnp.concatenate(picked, 0))


def prepare_kernel(groups, slots, vals, high_ref, low_ref, held, arrived):
    def fetch(g):
        return pltpu.make_async_copy(vals.at[:, pl.ds(8 * g, 8), :], held.at[g % 2], arrived.at[g % 2])

    fetch(0).start()
    for g in range(groups):
        if g + 1 < groups:
            fetch(g + 1).start()
        fetch(g).wait()
        for k in range(slots):
            block = jnp.concatenate([held[g % 2, k, :, 128 * t : 128 * t + 128] for t in range(32)], 0).T
            high, low = two_parts(block)
            high_ref[g, 128 * k : 128 * k + 128, :] = high.astype(BF16)
            low_ref[g, 128 * k : 128 * k + 128, :] = low.astype(BF16)


def prepare(vals):
    rows, slots, width = vals.shape
    shape = jax.ShapeDtypeStruct((rows // 8, 128 * slots, 256), BF16)
    return pl.pallas_call(
        functools.partial(prepare_kernel, rows // 8, slots),
        in_specs=[pl.BlockSpec(memory_space=pltpu.HBM)],
        out_specs=[VMEM, VMEM],
        out_shape=[shape, shape],
        scratch_shapes=[pltpu.VMEM((2, slots, 8, width), F32), pltpu.SemaphoreType.DMA((2,))],
        compiler_params=PARAMS,
        name="prepare",
    )(vals.transpose(1, 0, 2))


def prepare_transfer_kernel(vals, high_ref, low_ref, high_back_ref, low_back_ref):
    g = pl.program_id(0)
    block = jnp.concatenate([vals[:, 128 * t : 128 * t + 128] for t in range(32)], 0)
    high, low = two_parts(block)
    high_back_ref[g] = high.astype(BF16)
    low_back_ref[g] = low.astype(BF16)
    high, low = two_parts(block.T)
    high_ref[g] = high.astype(BF16)
    low_ref[g] = low.astype(BF16)


def prepare_transfer(vals):
    rows, width = vals.shape
    out = jax.ShapeDtypeStruct((rows // 8, 128, 256), BF16)
    back = jax.ShapeDtypeStruct((rows // 8, 256, 128), BF16)
    return pl.pallas_call(
        prepare_transfer_kernel,
        grid=(rows // 8,),
        in_specs=[pl.BlockSpec((8, width), lambda g: (g, 0))],
        out_specs=[VMEM] * 4,
        out_shape=[out, out, back, back],
        compiler_params=PARAMS,
        name="prepare_transfer",
    )(vals)


def restrict(prol_col, vector, high_ref, low_ref, total, partner_ref, own_ref, outer_ref):
    rows = masked_rows(vector)
    n = rows.shape[0]
    lane = lax.broadcasted_iota(jnp.int32, (128, 256), 0)
    pair = lax.broadcasted_iota(jnp.int32, (128, 256), 1) // 8
    gather = ((lane % 64) == 2 * pair + lane // 64).astype(F32).astype(BF16)
    pairs = jnp.dot(rows.reshape(16 * n, 128), gather, preferred_element_type=F32)
    lane16 = lax.broadcasted_iota(jnp.int32, (16, 256), 1) % 8
    total[...] = jnp.zeros_like(total)
    mask = same_half()[0]
    for g in range(n // 8):
        left = []
        for r in range(8):
            at = 128 * g + 16 * r
            left.append(jnp.where(lane16 == r, pairs[at : at + 16], 0.0))
        out = row_products(jnp.concatenate(left, 0).astype(BF16), high_ref, low_ref, g)
        for r in range(8):
            both = out[16 * r : 16 * r + 8] + out[16 * r + 8 : 16 * r + 16]
            c = prol_col[8 * g + r]
            total[c] = total[c] + jnp.where(mask, both, 0.0)
    whole = total[...]
    whole = whole + pltpu.roll(whole, 64, 2)
    whole = whole + other_row(whole)
    m = whole.shape[0] // 3
    partner_ref[...] = pack_halves(whole[:m])
    own_ref[...] = pack_halves(whole[m : 2 * m])
    outer_ref[...] = pack_halves(whole[2 * m :])


def smooth_kernel(step, count, col, own, partner, outer, high, low, resid, total, new_resid, new_d, new_total, window, left):
    fill_window(window, own, partner, outer)
    product = operator(lambda i, k: col[k - 1, i], 7, window, left, high, low, count)
    r = resid[...] - product
    d = step[0] * own[...] + step[1] * r
    new_resid[...] = r
    new_d[...] = d
    new_total[...] = total[...] + d


def restrict_kernel(
    count, col, prol_col, own, partner, outer, high, low, resid, back_high, back_low,
    new_resid, to_partner, to_own, to_outer, window, left, sums,
):
    fill_window(window, own, partner, outer)
    product = operator(lambda i, k: col[k - 1, i], 7, window, left, high, low, count)
    r = resid[...] - product
    new_resid[...] = r
    restrict(prol_col, r, back_high, back_low, sums, to_partner, to_own, to_outer)


def sum_kernel(own, partner, outer, total):
    total[...] = own[...] + partner[...] + outer[...]


def prolong_kernel(prol_col, own, partner, outer, high, low, total, spread, new_total, window, left):
    fill_window(window, own, partner, outer)
    product = operator(lambda i, k: prol_col[i], 1, window, left, high, low, None)
    spread[...] = product
    new_total[...] = total[...] + product


def resid_kernel(count, col, own, partner, outer, high, low, resid, total, new_resid, new_total, window, left):
    fill_window(window, own, partner, outer)
    product = operator(lambda i, k: col[k - 1, i], 7, window, left, high, low, count)
    r = resid[...] - product
    new_resid[...] = r
    new_total[...] = total[...] + r


def operator_scratch(window_blocks, rows, slots):
    return [pltpu.VMEM((window_blocks, 16, 128), BF16), pltpu.VMEM((16 * rows, 128 * slots), BF16)]


class Chain:
    last = None

    def __init__(self, active):
        self.active = active

    def call(self, kernel, name, scalars, vectors, outs, scratch):
        def guarded(active, previous, *refs):
            del previous

            @pl.when(active[0] != 0)
            def _():
                kernel(*refs)

        if Chain.last is None:
            Chain.last = vectors[0]
        results = pl.pallas_call(
            guarded,
            in_specs=[SMEM, pl.BlockSpec(memory_space=pl.ANY)] + [SMEM] * len(scalars) + [VMEM] * len(vectors),
            out_specs=[VMEM] * len(outs),
            out_shape=[jax.ShapeDtypeStruct((n // 2, 8, 128), F32) for n in outs],
            scratch_shapes=scratch,
            compiler_params=PARAMS,
            name=name,
        )(self.active, Chain.last, *scalars, *vectors)
        Chain.last = results[0]
        return results


def turns(steps):
    done = [0, 0]
    which, run = 0, 1
    while min(done) < steps:
        for _ in range(run):
            if done[which] < steps:
                yield which
                done[which] += 1
        which, run = 1 - which, 2


def to_packed(vector):
    half = vector.shape[0] // 2
    first, second = vector[:half], vector[half:]
    even = jnp.concatenate([first, second], -1)
    odd = jnp.concatenate([second, first], -1)
    return jnp.stack([even, odd], 2).reshape(half, 8, 128)


def from_packed(packed):
    split = packed.reshape(-1, 4, 2, 2, 64)
    return jnp.concatenate([split[:, :, 0, 0], split[:, :, 0, 1]], 0)


def body(right_side, fine_vals, fine_cols, prol_vals, prol_cols, coarse_vals, coarse_cols):
    devices = lax.axis_size("fine")
    rank = lax.axis_index("fine")
    n = right_side.shape[0]
    m = coarse_vals.shape[0]
    partner_rank = rank ^ 1

    def window_index(cols, per_device):
        owner = cols // per_device
        place = cols - owner * per_device
        slot = jnp.where(owner == rank, 1, jnp.where(owner == partner_rank, 0, 2))
        return (slot * per_device + place).astype(jnp.int32)

    fine_at = window_index(fine_cols.T, n)
    prol_at = window_index(prol_cols, m)
    coarse_at = window_index(coarse_cols.T, m)

    up = [(i, (i + 1) % devices) for i in range(devices)]
    down = [((i + 1) % devices, i) for i in range(devices)]
    inside = [(i, i ^ 1) for i in range(devices)]

    high, low = prepare(fine_vals)
    coarse_high, coarse_low = prepare(coarse_vals)
    prol_high, prol_low, back_high, back_low = prepare_transfer(prol_vals)
    first = to_packed(right_side)

    def steps(chain):
        def fine(kernel, name, d, more, outs, scalars=(), scratch=(), after=()):
            partner, outer = yield d, d
            vectors = (d, partner, outer, high, low, *more, *after)
            return chain.call(kernel, name, (fine_at, *scalars), vectors, outs, operator_scratch(3 * n, n, 7) + list(scratch))

        def fine_smooth(d, resid, total, step):
            kernel = functools.partial(smooth_kernel, step, n)
            return (yield from fine(kernel, "fine_smooth", d, (resid, total), [n, n, n]))

        def fine_resid(d, resid, total):
            kernel = functools.partial(resid_kernel, n)
            return (yield from fine(kernel, "fine_resid", d, (resid, total), [n, n]))

        def coarse_smooth(d, resid, total, step):
            partner, outer = yield d, d
            vectors = (d, partner, outer, coarse_high, coarse_low, resid, total)
            kernel = functools.partial(smooth_kernel, step, m)
            return chain.call(kernel, "coarse_smooth", (coarse_at,), vectors, [m, m, m], operator_scratch(3 * m, m, 7))

        def cycle(resid, total):
            resid, d, total = yield from fine_smooth(resid, resid, total, STEP1)
            resid, d, total = yield from fine_smooth(d, resid, total, STEP2)
            second, to_partner, to_own, to_outer = yield from fine(
                functools.partial(restrict_kernel, n), "fine_restrict", d, (resid,), [n, m, m, m],
                scalars=(prol_at,), scratch=[pltpu.VMEM((3 * m, 8, 128), F32)], after=(back_high, back_low),
            )
            partner, outer = yield to_partner, to_outer
            (right,) = chain.call(sum_kernel, "coarse_sum", (), (to_own, partner, outer), [m], [])
            resid, d, fix = yield from coarse_smooth(right, right, right, STEP1)
            resid, d, fix = yield from coarse_smooth(d, resid, fix, STEP2)
            partner, outer = yield fix, fix
            spread, total = chain.call(
                prolong_kernel, "prolong", (prol_at,),
                (fix, partner, outer, prol_high, prol_low, total), [n, n], operator_scratch(3 * m, n, 1),
            )
            resid, total = yield from fine_resid(spread, second, total)
            resid, d, total = yield from fine_smooth(resid, resid, total, STEP1)
            resid, d, total = yield from fine_smooth(d, resid, total, STEP2)
            return d, resid, total

        d, resid, total = yield from cycle(first, first)
        resid, total = yield from fine_resid(d, resid, total)
        d, resid, total = yield from cycle(resid, total)
        resid, _ = yield from fine_resid(d, resid, total)
        return total, resid

    odd = rank % 2
    Chain.last = None
    chains = [steps(Chain(jnp.reshape(odd, (1,)))), steps(Chain(jnp.reshape(1 - odd, (1,))))]
    for chain in chains:
        next(chain)
    from_left = lax.ppermute(first, "fine", up)
    from_right = lax.ppermute(first, "fine", down)
    inbox = [[(from_left, from_right)], [(from_right, from_left)]]
    results = [None, None]
    for which in turns(22):
        try:
            to_partner, to_outer = chains[which].send(inbox[which].pop(0))
        except StopIteration as end:
            results[which] = end.value
            continue
        outer = lax.ppermute(to_outer, "fine", (up, down)[which])
        partner = lax.ppermute(to_partner, "fine", inside)
        inbox[1 - which].append((partner, outer))
    total, resid = (jnp.where(odd != 0, a, b) for a, b in zip(*results))
    return from_packed(total), from_packed(resid)


def solution(mesh):
    in_specs = (
        P("fine", None, None),
        P("fine", None, None),
        P("fine", None),
        P("fine", None),
        P("fine"),
        P("fine", None, None),
        P("fine", None),
    )
    out_specs = (P("fine", None, None), P("fine", None, None))
    return jax.shard_map(body, mesh=mesh, in_specs=in_specs, out_specs=out_specs, check_vma=False)
```

```python
import functools

import jax
import jax.numpy as jnp
from jax import lax
from jax.experimental import pallas as pl
from jax.experimental.pallas import tpu as pltpu
from jax.sharding import PartitionSpec as P

THETA = 1.0
DELTA = 0.75
SIGMA = THETA / DELTA
RHO0 = 1.0 / SIGMA
RHO1 = 1.0 / (2.0 * SIGMA - RHO0)
RHO2 = 1.0 / (2.0 * SIGMA - RHO1)
STEP1 = (RHO1 * RHO0, 2.0 * RHO1 / DELTA)
STEP2 = (RHO2 * RHO1, 2.0 * RHO2 / DELTA)

F32 = jnp.float32
BF16 = jnp.bfloat16
VMEM = pl.BlockSpec(memory_space=pltpu.VMEM)
SMEM = pl.BlockSpec(memory_space=pltpu.SMEM)
PARAMS = pltpu.CompilerParams(vmem_limit_bytes=16 * 2**20)
STREAM_PARAMS = pltpu.CompilerParams(vmem_limit_bytes=48 * 2**20)


def same_half():
    row = lax.broadcasted_iota(jnp.int32, (1, 8, 128), 1)
    lane = lax.broadcasted_iota(jnp.int32, (1, 8, 128), 2)
    return (row // 4) == (lane // 64)


def first_rows():
    return lax.broadcasted_iota(jnp.int32, (1, 8, 128), 1) < 4


def other_row(x):
    return pltpu.roll(x, 4, 1)


def pack_halves(whole):
    half = whole.shape[0] // 2
    return jnp.where(same_half(), whole[:half], whole[half:])


def two_parts(x):
    high = x.astype(BF16).astype(F32)
    return high, x - high


def masked_rows(packed):
    mask = same_half()
    first = jnp.where(mask, packed, 0.0)
    second = pltpu.roll(jnp.where(mask, 0.0, packed), 64, 2)
    high, low = two_parts(jnp.concatenate([first, second], 0))
    return jnp.concatenate([high, low], 1).astype(BF16)


def own_lane(width):
    return lax.broadcasted_iota(jnp.int32, (8, width), 1) % 8


def from_pairs(rows):
    n = rows.shape[0]
    pair = lax.broadcasted_iota(jnp.int32, (256, 256), 0) // 8
    lane = lax.broadcasted_iota(jnp.int32, (256, 256), 1)
    spread = ((lane % 64) == 2 * pair + lane // 128).astype(F32).astype(BF16)
    high, low = two_parts(rows.reshape(n * 8, 256))
    both = jnp.concatenate([high, low], 0).astype(BF16)
    y = jnp.dot(both, spread, preferred_element_type=F32)
    y = (y[: n * 8] + y[n * 8 :]).reshape(n, 8, 256)
    y = jnp.where(first_rows(), y[:, :, :128], y[:, :, 128:])
    return pack_halves(y + other_row(y))


def row_products(left, high_ref, low_ref, group):
    out = jnp.dot(left, high_ref[group], preferred_element_type=F32)
    return out + jnp.dot(left, low_ref[group], preferred_element_type=F32)


def pick_rows(out):
    picked = []
    lane = own_lane(out.shape[1])
    for r in range(8):
        both = out[16 * r : 16 * r + 8] + out[16 * r + 8 : 16 * r + 16]
        picked.append(jnp.where(lane == r, both, 0.0)[None])
    return picked


def fill_window(window, own, partner, outer):
    n = 2 * own.shape[0]
    window[0:n] = masked_rows(partner[...])
    window[n : 2 * n] = masked_rows(own[...])
    window[2 * n : 3 * n] = masked_rows(outer[...])


def operator(col, slots, window, left, high_ref, low_ref, first):
    picked = []
    for g in range(high_ref.shape[0]):
        for i in range(8 * g, 8 * g + 8):
            for k in range(slots):
                at = first + i if (first is not None and k == 0) else col(i, k)
                left[16 * i : 16 * i + 16, 128 * k : 128 * k + 128] = window[at]
        out = row_products(left[128 * g : 128 * g + 128, 0 : 128 * slots], high_ref, low_ref, g)
        picked += pick_rows(out)
    return from_pairs(jnp.concatenate(picked, 0))


def prepare_kernel(groups, slots, rank, vals, high_ref, low_ref, held, arrived):
    del rank

    def fetch(g):
        return pltpu.make_async_copy(vals.at[:, pl.ds(8 * g, 8), :], held.at[g], arrived.at[g])

    for g in range(min(3, groups)):
        fetch(g).start()
    for g in range(groups):
        if g + 3 < groups:
            fetch(g + 3).start()
        fetch(g).wait()
        for k in range(slots):
            block = jnp.concatenate([held[g, k, :, 128 * t : 128 * t + 128] for t in range(32)], 0).T
            high, low = two_parts(block)
            high_ref[g, 128 * k : 128 * k + 128, :] = high.astype(BF16)
            low_ref[g, 128 * k : 128 * k + 128, :] = low.astype(BF16)


def prepare(rank, vals):
    rows, slots, width = vals.shape
    shape = pltpu.VMEM((rows // 8, 128 * slots, 256), BF16)
    return pl.pallas_call(
        functools.partial(prepare_kernel, rows // 8, slots),
        in_specs=[SMEM, pl.BlockSpec(memory_space=pltpu.HBM)],
        out_specs=[VMEM, VMEM],
        out_shape=[shape, shape],
        scratch_shapes=[pltpu.VMEM((rows // 8, slots, 8, width), F32), pltpu.SemaphoreType.DMA((rows // 8,))],
        compiler_params=STREAM_PARAMS if rows > 8 else PARAMS,
        name="prepare",
    )(rank, vals.transpose(1, 0, 2))


def prepare_transfer_kernel(vals, high_ref, low_ref, high_back_ref, low_back_ref):
    g = pl.program_id(0)
    block = jnp.concatenate([vals[:, 128 * t : 128 * t + 128] for t in range(32)], 0)
    high, low = two_parts(block)
    high_back_ref[g] = high.astype(BF16)
    low_back_ref[g] = low.astype(BF16)
    high, low = two_parts(block.T)
    high_ref[g] = high.astype(BF16)
    low_ref[g] = low.astype(BF16)


def prepare_transfer(vals):
    rows, width = vals.shape
    out = pltpu.VMEM((rows // 8, 128, 256), BF16)
    back = pltpu.VMEM((rows // 8, 256, 128), BF16)
    return pl.pallas_call(
        prepare_transfer_kernel,
        grid=(rows // 8,),
        in_specs=[pl.BlockSpec((8, width), lambda g: (g, 0))],
        out_specs=[VMEM] * 4,
        out_shape=[out, out, back, back],
        compiler_params=PARAMS,
        name="prepare_transfer",
    )(vals)


def restrict(prol_col, vector, high_ref, low_ref, total, partner_ref, own_ref, outer_ref):
    rows = masked_rows(vector)
    n = rows.shape[0]
    lane = lax.broadcasted_iota(jnp.int32, (128, 256), 0)
    pair = lax.broadcasted_iota(jnp.int32, (128, 256), 1) // 8
    gather = ((lane % 64) == 2 * pair + lane // 64).astype(F32).astype(BF16)
    pairs = jnp.dot(rows.reshape(16 * n, 128), gather, preferred_element_type=F32)
    lane16 = lax.broadcasted_iota(jnp.int32, (16, 256), 1) % 8
    total[...] = jnp.zeros_like(total)
    mask = same_half()[0]
    for g in range(n // 8):
        left = []
        for r in range(8):
            at = 128 * g + 16 * r
            left.append(jnp.where(lane16 == r, pairs[at : at + 16], 0.0))
        out = row_products(jnp.concatenate(left, 0).astype(BF16), high_ref, low_ref, g)
        for r in range(8):
            both = out[16 * r : 16 * r + 8] + out[16 * r + 8 : 16 * r + 16]
            c = prol_col[0, 8 * g + r]
            total[c] = total[c] + jnp.where(mask, both, 0.0)
    whole = total[...]
    whole = whole + pltpu.roll(whole, 64, 2)
    whole = whole + other_row(whole)
    m = whole.shape[0] // 3
    partner_ref[...] = pack_halves(whole[:m])
    own_ref[...] = pack_halves(whole[m : 2 * m])
    outer_ref[...] = pack_halves(whole[2 * m :])


def by_slot(col, i, k):
    return col[k - 1, i]


def by_row(col, i, k):
    return col[i, k - 1]


def smooth_kernel(step, count, at, col, own, outer, partner, high, low, resid, total, new_resid, new_d, new_total, window, left):
    fill_window(window, own, partner, outer)
    product = operator(functools.partial(at, col), 7, window, left, high, low, count)
    r = resid[...] - product
    d = step[0] * own[...] + step[1] * r
    new_resid[...] = r
    new_d[...] = d
    new_total[...] = total[...] + d


def restrict_kernel(
    count, col, prol_col, own, outer, partner, high, low, resid, back_high, back_low,
    new_resid, to_partner, to_own, to_outer, window, left, sums,
):
    fill_window(window, own, partner, outer)
    product = operator(functools.partial(by_slot, col), 7, window, left, high, low, count)
    r = resid[...] - product
    new_resid[...] = r
    restrict(prol_col, r, back_high, back_low, sums, to_partner, to_own, to_outer)


def sum_kernel(own, outer, partner, total):
    total[...] = own[...] + outer[...] + partner[...]


def prolong_kernel(prol_col, own, outer, partner, high, low, total, spread, new_total, window, left):
    fill_window(window, own, partner, outer)
    product = operator(lambda i, k: prol_col[0, i], 1, window, left, high, low, None)
    spread[...] = product
    new_total[...] = total[...] + product


def resid_kernel(count, col, own, outer, partner, high, low, resid, total, new_resid, new_total, window, left):
    fill_window(window, own, partner, outer)
    product = operator(functools.partial(by_slot, col), 7, window, left, high, low, count)
    r = resid[...] - product
    new_resid[...] = r
    new_total[...] = total[...] + r


def last_kernel(count, col, own, outer, partner, high, low, resid, total, *rest):
    *others, solution_out, resid_out, window, left = rest
    del others
    fill_window(window, own, partner, outer)
    product = operator(functools.partial(by_slot, col), 7, window, left, high, low, count)
    unpack_to(resid_out, resid[...] - product)
    unpack_to(solution_out, total[...])


def keep_others(*refs):
    other_solution, other_resid, solution_out, resid_out = refs[-6:-2]
    solution_out[...] = other_solution[...]
    resid_out[...] = other_resid[...]


def operator_scratch(window_blocks, rows, slots):
    return [pltpu.VMEM((window_blocks, 16, 128), BF16), pltpu.VMEM((16 * rows, 128 * slots), BF16)]


class Chain:
    last = None

    def __init__(self, rank, parity):
        self.rank = rank
        self.parity = parity

    def call(self, kernel, name, scalars, vectors, outs, scratch, otherwise=None):
        def guarded(rank, previous, *refs):
            del previous

            @pl.when((rank[0] & 1) == self.parity)
            def _():
                kernel(*refs)

            if otherwise is not None:

                @pl.when((rank[0] & 1) != self.parity)
                def _():
                    otherwise(*refs)

        if Chain.last is None:
            Chain.last = vectors[0]
        results = pl.pallas_call(
            guarded,
            in_specs=[SMEM, pl.BlockSpec(memory_space=pl.ANY)] + [SMEM] * len(scalars) + [VMEM] * len(vectors),
            out_specs=[VMEM] * len(outs),
            out_shape=[jax.ShapeDtypeStruct(out if isinstance(out, tuple) else (out // 2, 8, 128), F32) for out in outs],
            scratch_shapes=scratch,
            compiler_params=PARAMS,
            name=name,
        )(self.rank, Chain.last, *scalars, *vectors)
        Chain.last = results[0]
        return results


def turns(steps):
    done = [0, 0]
    which, run = 0, 1
    while min(done) < steps:
        for _ in range(run):
            if done[which] < steps:
                yield which
                done[which] += 1
        which, run = 1 - which, 2


def pack_kernel(rank, vector, packed):
    del rank
    half = vector.shape[0] // 2
    first, second = vector[:half], vector[half:]
    even = jnp.concatenate([first, second], -1)
    odd = jnp.concatenate([second, first], -1)
    packed[...] = jnp.concatenate([even, odd], 1)


def pack(rank, vector):
    blocks, sides, width = vector.shape
    return pl.pallas_call(
        pack_kernel,
        in_specs=[SMEM, VMEM],
        out_specs=VMEM,
        out_shape=jax.ShapeDtypeStruct((blocks // 2, 2 * sides, 2 * width), F32),
        compiler_params=PARAMS,
        name="pack",
    )(rank, vector)


def unpack_to(out, packed):
    half = packed.shape[0]
    out[:half] = packed[:, :4, :64]
    out[half:] = packed[:, :4, 64:]


def window_index_kernel(n, m, rank, fine, prol, coarse, *refs):
    for i, (cols, per_device) in enumerate(((fine, n), (prol, m), (coarse, m))):
        out, held, sem = refs[i], refs[3 + i], refs[6 + i]
        place = cols[...] - rank[0] * per_device
        inner = cols[...] - (rank[0] ^ 1) * per_device
        there = lax.rem(cols[...], per_device) + 2 * per_device
        here = (place >= 0) & (place < per_device)
        beside = (inner >= 0) & (inner < per_device)
        held[...] = jnp.where(here, place + per_device, jnp.where(beside, inner, there))
        pltpu.make_async_copy(held, out, sem).start()
    for i in range(3):
        pltpu.make_async_copy(refs[3 + i], refs[i], refs[6 + i]).wait()


def window_index(n, m, rank, *cols):
    return pl.pallas_call(
        functools.partial(window_index_kernel, n, m),
        in_specs=[SMEM] + [VMEM] * len(cols),
        out_specs=[SMEM] * len(cols),
        out_shape=[pltpu.SMEM(c.shape, jnp.int32) for c in cols],
        scratch_shapes=[pltpu.VMEM(c.shape, jnp.int32) for c in cols] + [pltpu.SemaphoreType.DMA] * len(cols),
        compiler_params=PARAMS,
        name="window_index",
    )(rank, *cols)


def body(right_side, fine_vals, fine_cols, prol_vals, prol_cols, coarse_vals, coarse_cols):
    devices = lax.axis_size("fine")
    rank = jnp.reshape(lax.axis_index("fine"), (1,))
    n = right_side.shape[0]
    m = coarse_vals.shape[0]

    first = pack(rank, right_side)
    fine_at, prol_at, coarse_at = window_index(
        n, m, rank, fine_cols.T, prol_cols.reshape(1, n), coarse_cols
    )
    up = [(i, (i + 1) % devices) for i in range(devices)]
    down = [((i + 1) % devices, i) for i in range(devices)]
    inside = [(i, i ^ 1) for i in range(devices)]
    across = [(i, (i + 1 if i % 2 else i - 1) % devices) for i in range(devices)]

    high, low = prepare(rank, fine_vals)
    coarse_high, coarse_low = prepare(rank, coarse_vals)
    prol_high, prol_low, back_high, back_low = prepare_transfer(prol_vals)

    def steps(chain):
        def fine(kernel, name, d, more, outs, scalars=(), scratch=(), after=()):
            partner, outer = yield d, d
            vectors = (d, outer, partner, high, low, *more, *after)
            return chain.call(kernel, name, (fine_at, *scalars), vectors, outs, operator_scratch(3 * n, n, 7) + list(scratch))

        def fine_smooth(d, resid, total, step):
            kernel = functools.partial(smooth_kernel, step, n, by_slot)
            return (yield from fine(kernel, "fine_smooth", d, (resid, total), [n, n, n]))

        def fine_resid(d, resid, total):
            kernel = functools.partial(resid_kernel, n)
            return (yield from fine(kernel, "fine_resid", d, (resid, total), [n, n]))

        def coarse_smooth(d, resid, total, step):
            partner, outer = yield d, d
            vectors = (d, outer, partner, coarse_high, coarse_low, resid, total)
            kernel = functools.partial(smooth_kernel, step, m, by_row)
            return chain.call(kernel, "coarse_smooth", (coarse_at,), vectors, [m, m, m], operator_scratch(3 * m, m, 7))

        def cycle(resid, total):
            resid, d, total = yield from fine_smooth(resid, resid, total, STEP1)
            resid, d, total = yield from fine_smooth(d, resid, total, STEP2)
            second, to_partner, to_own, to_outer = yield from fine(
                functools.partial(restrict_kernel, n), "fine_restrict", d, (resid,), [n, m, m, m],
                scalars=(prol_at,), scratch=[pltpu.VMEM((3 * m, 8, 128), F32)], after=(back_high, back_low),
            )
            partner, outer = yield to_partner, to_outer
            (right,) = chain.call(sum_kernel, "coarse_sum", (), (to_own, outer, partner), [m], [])
            resid, d, fix = yield from coarse_smooth(right, right, right, STEP1)
            resid, d, fix = yield from coarse_smooth(d, resid, fix, STEP2)
            partner, outer = yield fix, fix
            spread, total = chain.call(
                prolong_kernel, "prolong", (prol_at,),
                (fix, outer, partner, prol_high, prol_low, total), [n, n], operator_scratch(3 * m, n, 1),
            )
            resid, total = yield from fine_resid(spread, second, total)
            resid, d, total = yield from fine_smooth(resid, resid, total, STEP1)
            resid, d, total = yield from fine_smooth(d, resid, total, STEP2)
            return d, resid, total

        d, resid, total = yield from cycle(first, first)
        resid, total = yield from fine_resid(d, resid, total)
        d, resid, total = yield from cycle(resid, total)
        partner, outer = yield d, d
        vectors = (d, outer, partner, high, low, resid, total, *finished)
        finished[:] = chain.call(
            functools.partial(last_kernel, n), "fine_last", (fine_at,), vectors,
            [right_side.shape] * 2, operator_scratch(3 * n, n, 7), keep_others if finished else None,
        )

    finished = []
    Chain.last = None
    chains = [steps(Chain(rank, 1)), steps(Chain(rank, 0))]
    for chain in chains:
        next(chain)
    arrived = (lax.ppermute(first, "fine", inside), lax.ppermute(first, "fine", across))
    inbox = [[arrived], [arrived]]
    for which in turns(22):
        try:
            to_partner, to_outer = chains[which].send(inbox[which].pop(0))
        except StopIteration:
            continue
        partner = lax.ppermute(to_partner, "fine", inside)
        outer = lax.ppermute(to_outer, "fine", (up, down)[which])
        inbox[1 - which].append((partner, outer))
    return tuple(finished)


def solution(mesh):
    in_specs = (
        P("fine", None, None),
        P("fine", None, None),
        P("fine", None),
        P("fine", None),
        P("fine"),
        P("fine", None, None),
        P("fine", None),
    )
    out_specs = (P("fine", None, None), P("fine", None, None))
    return jax.shard_map(body, mesh=mesh, in_specs=in_specs, out_specs=out_specs, check_vma=False)
```

```python
import functools

import jax
import jax.numpy as jnp
from jax import lax
from jax.experimental import pallas as pl
from jax.experimental.pallas import tpu as pltpu
from jax.sharding import PartitionSpec as P

THETA = 1.0
DELTA = 0.75
SIGMA = THETA / DELTA
RHO0 = 1.0 / SIGMA
RHO1 = 1.0 / (2.0 * SIGMA - RHO0)
RHO2 = 1.0 / (2.0 * SIGMA - RHO1)
STEP1 = (RHO1 * RHO0, 2.0 * RHO1 / DELTA)
STEP2 = (RHO2 * RHO1, 2.0 * RHO2 / DELTA)

F32 = jnp.float32
BF16 = jnp.bfloat16
VMEM = pl.BlockSpec(memory_space=pltpu.VMEM)
SMEM = pl.BlockSpec(memory_space=pltpu.SMEM)
PARAMS = pltpu.CompilerParams(vmem_limit_bytes=16 * 2**20)
STREAM_PARAMS = pltpu.CompilerParams(vmem_limit_bytes=48 * 2**20)


def halves():
    row = lax.broadcasted_iota(jnp.int32, (1, 8, 128), 1)
    lane = lax.broadcasted_iota(jnp.int32, (1, 8, 128), 2)
    return row < 4, lane < 64


def corners():
    top, front = halves()
    return top & front, jnp.logical_not(top | front)


def other_row(x):
    return pltpu.roll(x, 4, 1)


def other_lane(x):
    return pltpu.roll(x, 64, 2)


def pack_quarters(whole):
    top, front = halves()
    q = whole.shape[0] // 4
    first = jnp.where(front, whole[:q], whole[2 * q : 3 * q])
    return jnp.where(top, first, jnp.where(front, whole[3 * q :], whole[q : 2 * q]))


def two_parts(x):
    high = x.astype(BF16).astype(F32)
    return high, x - high


def masked_rows(packed):
    first, last = corners()
    lanes = other_lane(packed)
    rows = other_row(packed)
    both = other_row(lanes)
    blocks = [
        jnp.where(first, packed, jnp.where(last, both, 0.0)),
        jnp.where(last, packed, jnp.where(first, both, 0.0)),
        jnp.where(first, lanes, jnp.where(last, rows, 0.0)),
        jnp.where(last, lanes, jnp.where(first, rows, 0.0)),
    ]
    high, low = two_parts(jnp.concatenate(blocks, 0))
    return jnp.concatenate([high, low], 1).astype(BF16)


def own_lane(width):
    return lax.broadcasted_iota(jnp.int32, (8, width), 1) % 8


def from_pairs(rows):
    n = rows.shape[0]
    pair = lax.broadcasted_iota(jnp.int32, (256, 256), 0) // 8
    lane = lax.broadcasted_iota(jnp.int32, (256, 256), 1)
    spread = ((lane % 64) == 2 * pair + lane // 128).astype(F32).astype(BF16)
    high, low = two_parts(rows.reshape(n * 8, 256))
    both = jnp.concatenate([high, low], 0).astype(BF16)
    y = jnp.dot(both, spread, preferred_element_type=F32)
    y = (y[: n * 8] + y[n * 8 :]).reshape(n, 8, 256)
    y = jnp.where(halves()[0], y[:, :, :128], y[:, :, 128:])
    return pack_quarters(y + other_row(y))


def row_products(left, high_ref, low_ref, group):
    out = jnp.dot(left, high_ref[group], preferred_element_type=F32)
    return out + jnp.dot(left, low_ref[group], preferred_element_type=F32)


def pick_rows(out):
    picked = []
    lane = own_lane(out.shape[1])
    for r in range(8):
        both = out[16 * r : 16 * r + 8] + out[16 * r + 8 : 16 * r + 16]
        picked.append(jnp.where(lane == r, both, 0.0)[None])
    return picked


def fill_window(window, own, partner, outer):
    n = 4 * own.shape[0]
    window[0:n] = masked_rows(partner[...])
    window[n : 2 * n] = masked_rows(own[...])
    window[2 * n : 3 * n] = masked_rows(outer[...])


def operator(col, slots, window, left, high_ref, low_ref, first):
    picked = []
    for g in range(high_ref.shape[0]):
        for i in range(8 * g, 8 * g + 8):
            for k in range(slots):
                at = first + i if (first is not None and k == 0) else col(i, k)
                left[16 * i : 16 * i + 16, 128 * k : 128 * k + 128] = window[at]
        out = row_products(left[128 * g : 128 * g + 128, 0 : 128 * slots], high_ref, low_ref, g)
        picked += pick_rows(out)
    return from_pairs(jnp.concatenate(picked, 0))


def prepare_kernel(groups, slots, rank, vals, high_ref, low_ref, held, arrived):
    del rank

    def fetch(g):
        return pltpu.make_async_copy(vals.at[:, pl.ds(8 * g, 8), :], held.at[g], arrived.at[g])

    for g in range(min(3, groups)):
        fetch(g).start()
    for g in range(groups):
        if g + 3 < groups:
            fetch(g + 3).start()
        fetch(g).wait()
        for k in range(slots):
            block = jnp.concatenate([held[g, k, :, 128 * t : 128 * t + 128] for t in range(32)], 0).T
            high, low = two_parts(block)
            high_ref[g, 128 * k : 128 * k + 128, :] = high.astype(BF16)
            low_ref[g, 128 * k : 128 * k + 128, :] = low.astype(BF16)


def prepare(rank, vals):
    rows, slots, width = vals.shape
    shape = pltpu.VMEM((rows // 8, 128 * slots, 256), BF16)
    return pl.pallas_call(
        functools.partial(prepare_kernel, rows // 8, slots),
        in_specs=[SMEM, pl.BlockSpec(memory_space=pltpu.HBM)],
        out_specs=[VMEM, VMEM],
        out_shape=[shape, shape],
        scratch_shapes=[pltpu.VMEM((rows // 8, slots, 8, width), F32), pltpu.SemaphoreType.DMA((rows // 8,))],
        compiler_params=STREAM_PARAMS if rows > 8 else PARAMS,
        name="prepare",
    )(rank, vals.transpose(1, 0, 2))


def prepare_transfer_kernel(vals, high_ref, low_ref, high_back_ref, low_back_ref):
    g = pl.program_id(0)
    block = jnp.concatenate([vals[:, 128 * t : 128 * t + 128] for t in range(32)], 0)
    high, low = two_parts(block)
    high_back_ref[g] = high.astype(BF16)
    low_back_ref[g] = low.astype(BF16)
    high, low = two_parts(block.T)
    high_ref[g] = high.astype(BF16)
    low_ref[g] = low.astype(BF16)


def prepare_transfer(vals):
    rows, width = vals.shape
    out = pltpu.VMEM((rows // 8, 128, 256), BF16)
    back = pltpu.VMEM((rows // 8, 256, 128), BF16)
    return pl.pallas_call(
        prepare_transfer_kernel,
        grid=(rows // 8,),
        in_specs=[pl.BlockSpec((8, width), lambda g: (g, 0))],
        out_specs=[VMEM] * 4,
        out_shape=[out, out, back, back],
        compiler_params=PARAMS,
        name="prepare_transfer",
    )(vals)


def restrict(prol_col, vector, high_ref, low_ref, total, partner_ref, own_ref, outer_ref):
    rows = masked_rows(vector)
    n = rows.shape[0]
    lane = lax.broadcasted_iota(jnp.int32, (128, 256), 0)
    pair = lax.broadcasted_iota(jnp.int32, (128, 256), 1) // 8
    gather = ((lane % 64) == 2 * pair + lane // 64).astype(F32).astype(BF16)
    pairs = jnp.dot(rows.reshape(16 * n, 128), gather, preferred_element_type=F32)
    lane16 = lax.broadcasted_iota(jnp.int32, (16, 256), 1) % 8
    total[...] = jnp.zeros_like(total)
    first, last = corners()
    mask = (first | last)[0]
    for g in range(n // 8):
        left = []
        for r in range(8):
            at = 128 * g + 16 * r
            left.append(jnp.where(lane16 == r, pairs[at : at + 16], 0.0))
        out = row_products(jnp.concatenate(left, 0).astype(BF16), high_ref, low_ref, g)
        for r in range(8):
            both = out[16 * r : 16 * r + 8] + out[16 * r + 8 : 16 * r + 16]
            c = prol_col[0, 8 * g + r]
            total[c] = total[c] + jnp.where(mask, both, 0.0)
    whole = total[...]
    whole = whole + other_lane(whole)
    whole = whole + other_row(whole)
    m = whole.shape[0] // 3
    partner_ref[...] = pack_quarters(whole[:m])
    own_ref[...] = pack_quarters(whole[m : 2 * m])
    outer_ref[...] = pack_quarters(whole[2 * m :])


def by_slot(col, i, k):
    return col[k - 1, i]


def by_row(col, i, k):
    return col[i, k - 1]


def smooth_kernel(step, count, at, col, own, outer, partner, high, low, resid, total, new_resid, new_d, new_total, window, left):
    fill_window(window, own, partner, outer)
    product = operator(functools.partial(at, col), 7, window, left, high, low, count)
    r = resid[...] - product
    d = step[0] * own[...] + step[1] * r
    new_resid[...] = r
    new_d[...] = d
    new_total[...] = total[...] + d


def total_kernel(step, count, at, col, own, outer, partner, high, low, resid, total, new_total, window, left):
    fill_window(window, own, partner, outer)
    product = operator(functools.partial(at, col), 7, window, left, high, low, count)
    new_total[...] = total[...] + step[0] * own[...] + step[1] * (resid[...] - product)


def restrict_kernel(
    count, col, prol_col, own, outer, partner, high, low, resid, back_high, back_low,
    new_resid, to_partner, to_own, to_outer, window, left, sums,
):
    fill_window(window, own, partner, outer)
    product = operator(functools.partial(by_slot, col), 7, window, left, high, low, count)
    r = resid[...] - product
    new_resid[...] = r
    restrict(prol_col, r, back_high, back_low, sums, to_partner, to_own, to_outer)


def sum_kernel(own, outer, partner, total):
    total[...] = own[...] + outer[...] + partner[...]


def prolong_kernel(prol_col, own, outer, partner, high, low, total, spread, new_total, window, left):
    fill_window(window, own, partner, outer)
    product = operator(lambda i, k: prol_col[0, i], 1, window, left, high, low, None)
    spread[...] = product
    new_total[...] = total[...] + product


def resid_kernel(count, col, own, outer, partner, high, low, resid, total, new_resid, new_total, window, left):
    fill_window(window, own, partner, outer)
    product = operator(functools.partial(by_slot, col), 7, window, left, high, low, count)
    r = resid[...] - product
    new_resid[...] = r
    new_total[...] = total[...] + r


def last_kernel(count, col, own, outer, partner, high, low, resid, total, *rest):
    *others, solution_out, resid_out, window, left = rest
    del others
    fill_window(window, own, partner, outer)
    product = operator(functools.partial(by_slot, col), 7, window, left, high, low, count)
    unpack_to(resid_out, resid[...] - product)
    unpack_to(solution_out, total[...])


def keep_others(*refs):
    other_solution, other_resid, solution_out, resid_out = refs[-6:-2]
    solution_out[...] = other_solution[...]
    resid_out[...] = other_resid[...]


def operator_scratch(window_blocks, rows, slots):
    return [pltpu.VMEM((window_blocks, 16, 128), BF16), pltpu.VMEM((16 * rows, 128 * slots), BF16)]


class Chain:
    last = None

    def __init__(self, rank, parity):
        self.rank = rank
        self.parity = parity

    def call(self, kernel, name, scalars, vectors, outs, scratch, otherwise=None):
        def guarded(rank, previous, *refs):
            del previous

            @pl.when((rank[0] & 1) == self.parity)
            def _():
                kernel(*refs)

            if otherwise is not None:

                @pl.when((rank[0] & 1) != self.parity)
                def _():
                    otherwise(*refs)

        if Chain.last is None:
            Chain.last = vectors[0]
        results = pl.pallas_call(
            guarded,
            in_specs=[SMEM, pl.BlockSpec(memory_space=pl.ANY)] + [SMEM] * len(scalars) + [VMEM] * len(vectors),
            out_specs=[VMEM] * len(outs),
            out_shape=[
                jax.ShapeDtypeStruct(out, F32) if isinstance(out, tuple) else pltpu.VMEM((out // 4, 8, 128), F32)
                for out in outs
            ],
            scratch_shapes=scratch,
            compiler_params=PARAMS,
            name=name,
        )(self.rank, Chain.last, *scalars, *vectors)
        Chain.last = results[0]
        return results


def turns(steps):
    done = [0, 0]
    which, run = 0, 1
    while min(done) < steps:
        for _ in range(run):
            if done[which] < steps:
                yield which
                done[which] += 1
        which, run = 1 - which, 2


def pack_kernel(rank, vector, packed):
    del rank
    q = vector.shape[0] // 4
    top = jnp.concatenate([vector[:q], vector[2 * q : 3 * q]], -1)
    bottom = jnp.concatenate([vector[3 * q :], vector[q : 2 * q]], -1)
    packed[...] = jnp.concatenate([top, bottom], 1)


def pack(rank, vector):
    blocks, sides, width = vector.shape
    return pl.pallas_call(
        pack_kernel,
        in_specs=[SMEM, VMEM],
        out_specs=VMEM,
        out_shape=jax.ShapeDtypeStruct((blocks // 4, 2 * sides, 2 * width), F32),
        compiler_params=PARAMS,
        name="pack",
    )(rank, vector)


def unpack_to(out, packed):
    q = packed.shape[0]
    out[:q] = packed[:, :4, :64]
    out[q : 2 * q] = packed[:, 4:, 64:]
    out[2 * q : 3 * q] = packed[:, :4, 64:]
    out[3 * q :] = packed[:, 4:, :64]


def window_index_kernel(n, m, rank, fine, prol, coarse, *refs):
    for i, (cols, per_device) in enumerate(((fine, n), (prol, m), (coarse, m))):
        out, held, sem = refs[i], refs[3 + i], refs[6 + i]
        place = cols[...] - rank[0] * per_device
        inner = cols[...] - (rank[0] ^ 1) * per_device
        there = lax.rem(cols[...], per_device) + 2 * per_device
        here = (place >= 0) & (place < per_device)
        beside = (inner >= 0) & (inner < per_device)
        held[...] = jnp.where(here, place + per_device, jnp.where(beside, inner, there))
        pltpu.make_async_copy(held, out, sem).start()
    for i in range(3):
        pltpu.make_async_copy(refs[3 + i], refs[i], refs[6 + i]).wait()


def window_index(n, m, rank, *cols):
    return pl.pallas_call(
        functools.partial(window_index_kernel, n, m),
        in_specs=[SMEM] + [VMEM] * len(cols),
        out_specs=[SMEM] * len(cols),
        out_shape=[pltpu.SMEM(c.shape, jnp.int32) for c in cols],
        scratch_shapes=[pltpu.VMEM(c.shape, jnp.int32) for c in cols] + [pltpu.SemaphoreType.DMA] * len(cols),
        compiler_params=PARAMS,
        name="window_index",
    )(rank, *cols)


def body(right_side, fine_vals, fine_cols, prol_vals, prol_cols, coarse_vals, coarse_cols):
    devices = lax.axis_size("fine")
    rank = jnp.reshape(lax.axis_index("fine"), (1,))
    n = right_side.shape[0]
    m = coarse_vals.shape[0]

    first = pack(rank, right_side)
    fine_at, prol_at, coarse_at = window_index(
        n, m, rank, fine_cols.T, prol_cols.reshape(1, n), coarse_cols
    )
    up = [(i, (i + 1) % devices) for i in range(devices)]
    down = [((i + 1) % devices, i) for i in range(devices)]
    inside = [(i, i ^ 1) for i in range(devices)]
    across = [(i, (i + 1 if i % 2 else i - 1) % devices) for i in range(devices)]

    high, low = prepare(rank, fine_vals)
    coarse_high, coarse_low = prepare(rank, coarse_vals)
    prol_high, prol_low, back_high, back_low = prepare_transfer(prol_vals)

    def steps(chain):
        def fine(kernel, name, d, more, outs, scalars=(), scratch=(), after=()):
            partner, outer = yield d, d
            vectors = (d, outer, partner, high, low, *more, *after)
            return chain.call(kernel, name, (fine_at, *scalars), vectors, outs, operator_scratch(3 * n, n, 7) + list(scratch))

        def fine_smooth(d, resid, total, step):
            kernel = functools.partial(smooth_kernel, step, n, by_slot)
            return (yield from fine(kernel, "fine_smooth", d, (resid, total), [n, n, n]))

        def fine_resid(d, resid, total):
            kernel = functools.partial(resid_kernel, n)
            return (yield from fine(kernel, "fine_resid", d, (resid, total), [n, n]))

        def coarse(kernel, name, d, resid, total, step, outs):
            partner, outer = yield d, d
            vectors = (d, outer, partner, coarse_high, coarse_low, resid, total)
            kernel = functools.partial(kernel, step, m, by_row)
            return chain.call(kernel, name, (coarse_at,), vectors, outs, operator_scratch(3 * m, m, 7))

        def cycle(resid, total):
            resid, d, total = yield from fine_smooth(resid, resid, total, STEP1)
            resid, d, total = yield from fine_smooth(d, resid, total, STEP2)
            second, to_partner, to_own, to_outer = yield from fine(
                functools.partial(restrict_kernel, n), "fine_restrict", d, (resid,), [n, m, m, m],
                scalars=(prol_at,), scratch=[pltpu.VMEM((3 * m, 8, 128), F32)], after=(back_high, back_low),
            )
            partner, outer = yield to_partner, to_outer
            (right,) = chain.call(sum_kernel, "coarse_sum", (), (to_own, outer, partner), [m], [])
            resid, d, fix = yield from coarse(smooth_kernel, "coarse_smooth", right, right, right, STEP1, [m, m, m])
            (fix,) = yield from coarse(total_kernel, "coarse_total", d, resid, fix, STEP2, [m])
            partner, outer = yield fix, fix
            spread, total = chain.call(
                prolong_kernel, "prolong", (prol_at,),
                (fix, outer, partner, prol_high, prol_low, total), [n, n], operator_scratch(3 * m, n, 1),
            )
            resid, total = yield from fine_resid(spread, second, total)
            resid, d, total = yield from fine_smooth(resid, resid, total, STEP1)
            resid, d, total = yield from fine_smooth(d, resid, total, STEP2)
            return d, resid, total

        d, resid, total = yield from cycle(first, first)
        resid, total = yield from fine_resid(d, resid, total)
        d, resid, total = yield from cycle(resid, total)
        partner, outer = yield d, d
        vectors = (d, outer, partner, high, low, resid, total, *finished)
        finished[:] = chain.call(
            functools.partial(last_kernel, n), "fine_last", (fine_at,), vectors,
            [right_side.shape] * 2, operator_scratch(3 * n, n, 7), keep_others if finished else None,
        )

    finished = []
    Chain.last = None
    chains = [steps(Chain(rank, 1)), steps(Chain(rank, 0))]
    for chain in chains:
        next(chain)
    arrived = (lax.ppermute(first, "fine", inside), lax.ppermute(first, "fine", across))
    inbox = [[arrived], [arrived]]
    for which in turns(22):
        try:
            to_partner, to_outer = chains[which].send(inbox[which].pop(0))
        except StopIteration:
            continue
        partner = lax.ppermute(to_partner, "fine", inside)
        outer = lax.ppermute(to_outer, "fine", (up, down)[which])
        inbox[1 - which].append((partner, outer))
    return tuple(finished)


def solution(mesh):
    in_specs = (
        P("fine", None, None),
        P("fine", None, None),
        P("fine", None),
        P("fine", None),
        P("fine"),
        P("fine", None, None),
        P("fine", None),
    )
    out_specs = (P("fine", None, None), P("fine", None, None))
    return jax.shard_map(body, mesh=mesh, in_specs=in_specs, out_specs=out_specs, check_vma=False)
```

```python
import functools

import jax
import jax.numpy as jnp
from jax import lax
from jax.experimental import pallas as pl
from jax.experimental.pallas import tpu as pltpu
from jax.sharding import PartitionSpec as P

THETA = 1.0
DELTA = 0.75
SIGMA = THETA / DELTA
RHO0 = 1.0 / SIGMA
RHO1 = 1.0 / (2.0 * SIGMA - RHO0)
RHO2 = 1.0 / (2.0 * SIGMA - RHO1)
STEP1 = (RHO1 * RHO0, 2.0 * RHO1 / DELTA)
STEP2 = (RHO2 * RHO1, 2.0 * RHO2 / DELTA)

F32 = jnp.float32
BF16 = jnp.bfloat16
VMEM = pl.BlockSpec(memory_space=pltpu.VMEM)
SMEM = pl.BlockSpec(memory_space=pltpu.SMEM)
PARAMS = pltpu.CompilerParams(vmem_limit_bytes=16 * 2**20)
STREAM_PARAMS = pltpu.CompilerParams(vmem_limit_bytes=48 * 2**20)


def halves():
    row = lax.broadcasted_iota(jnp.int32, (1, 8, 128), 1)
    lane = lax.broadcasted_iota(jnp.int32, (1, 8, 128), 2)
    return row < 4, lane < 64


def corners():
    top, front = halves()
    return top & front, jnp.logical_not(top | front)


def other_row(x):
    return pltpu.roll(x, 4, 1)


def other_lane(x):
    return pltpu.roll(x, 64, 2)


def pack_quarters(whole):
    top, front = halves()
    q = whole.shape[0] // 4
    first = jnp.where(front, whole[:q], whole[2 * q : 3 * q])
    return jnp.where(top, first, jnp.where(front, whole[3 * q :], whole[q : 2 * q]))


def two_parts(x):
    high = x.astype(BF16).astype(F32)
    return high, x - high


def masked_rows(packed):
    first, last = corners()
    lanes = other_lane(packed)
    rows = other_row(packed)
    both = other_row(lanes)
    blocks = [
        jnp.where(first, packed, jnp.where(last, both, 0.0)),
        jnp.where(last, packed, jnp.where(first, both, 0.0)),
        jnp.where(first, lanes, jnp.where(last, rows, 0.0)),
        jnp.where(last, lanes, jnp.where(first, rows, 0.0)),
    ]
    high, low = two_parts(jnp.concatenate(blocks, 0))
    return jnp.concatenate([high, low], 1).astype(BF16)


def own_lane(width):
    return lax.broadcasted_iota(jnp.int32, (8, width), 1) % 8


def from_pairs(rows):
    n = rows.shape[0]
    pair = lax.broadcasted_iota(jnp.int32, (256, 256), 0) // 8
    lane = lax.broadcasted_iota(jnp.int32, (256, 256), 1)
    spread = ((lane % 64) == 2 * pair + lane // 128).astype(F32).astype(BF16)
    high, low = two_parts(rows.reshape(n * 8, 256))
    both = jnp.concatenate([high, low], 0).astype(BF16)
    y = jnp.dot(both, spread, preferred_element_type=F32)
    y = (y[: n * 8] + y[n * 8 :]).reshape(n, 8, 256)
    y = jnp.where(halves()[0], y[:, :, :128], y[:, :, 128:])
    return pack_quarters(y + other_row(y))


def row_products(left, high_ref, low_ref, group):
    out = jnp.dot(left, high_ref[group], preferred_element_type=F32)
    return out + jnp.dot(left, low_ref[group], preferred_element_type=F32)


def pick_rows(out):
    picked = []
    lane = own_lane(out.shape[1])
    for r in range(8):
        both = out[16 * r : 16 * r + 8] + out[16 * r + 8 : 16 * r + 16]
        picked.append(jnp.where(lane == r, both, 0.0)[None])
    return picked


def fill_window(window, own, partner, outer):
    n = 4 * own.shape[0]
    window[0:n] = masked_rows(partner[...])
    window[n : 2 * n] = masked_rows(own[...])
    window[2 * n : 3 * n] = masked_rows(outer[...])


def operator_pairs(col, slots, window, left, high_ref, low_ref, first):
    picked = []
    for g in range(high_ref.shape[0]):
        for i in range(8 * g, 8 * g + 8):
            for k in range(slots):
                at = first + i if (first is not None and k == 0) else col(i, k)
                left[16 * i : 16 * i + 16, 128 * k : 128 * k + 128] = window[at]
        out = row_products(left[128 * g : 128 * g + 128, 0 : 128 * slots], high_ref, low_ref, g)
        picked += pick_rows(out)
    return jnp.concatenate(picked, 0)


def operator(*args):
    return from_pairs(operator_pairs(*args))


def split_groups(groups, slots, vals, high_ref, low_ref, held, arrived, meanwhile=None):
    def fetch(g):
        return pltpu.make_async_copy(vals.at[:, pl.ds(8 * g, 8), :], held.at[g], arrived.at[g])

    for g in range(min(3, groups)):
        fetch(g).start()
    if meanwhile is not None:
        meanwhile()
    for g in range(groups):
        if g + 3 < groups:
            fetch(g + 3).start()
        fetch(g).wait()
        for k in range(slots):
            block = jnp.concatenate([held[g, k, :, 128 * t : 128 * t + 128] for t in range(32)], 0).T
            high, low = two_parts(block)
            high_ref[g, 128 * k : 128 * k + 128, :] = high.astype(BF16)
            low_ref[g, 128 * k : 128 * k + 128, :] = low.astype(BF16)


def prepare_kernel(groups, slots, rank, *refs):
    del rank
    split_groups(groups, slots, *refs)


def prepare(rank, vals):
    rows, slots, width = vals.shape
    shape = pltpu.VMEM((rows // 8, 128 * slots, 256), BF16)
    return pl.pallas_call(
        functools.partial(prepare_kernel, rows // 8, slots),
        in_specs=[SMEM, pl.BlockSpec(memory_space=pltpu.HBM)],
        out_specs=[VMEM, VMEM],
        out_shape=[shape, shape],
        scratch_shapes=[pltpu.VMEM((rows // 8, slots, 8, width), F32), pltpu.SemaphoreType.DMA((rows // 8,))],
        compiler_params=PARAMS,
        name="prepare",
    )(rank, vals.transpose(1, 0, 2))


def prepare_transfer_kernel(vals, high_ref, low_ref, high_back_ref, low_back_ref):
    g = pl.program_id(0)
    block = jnp.concatenate([vals[:, 128 * t : 128 * t + 128] for t in range(32)], 0)
    high, low = two_parts(block)
    high_back_ref[g] = high.astype(BF16)
    low_back_ref[g] = low.astype(BF16)
    high, low = two_parts(block.T)
    high_ref[g] = high.astype(BF16)
    low_ref[g] = low.astype(BF16)


def prepare_transfer(vals):
    rows, width = vals.shape
    out = pltpu.VMEM((rows // 8, 128, 256), BF16)
    back = pltpu.VMEM((rows // 8, 256, 128), BF16)
    return pl.pallas_call(
        prepare_transfer_kernel,
        grid=(rows // 8,),
        in_specs=[pl.BlockSpec((8, width), lambda g: (g, 0))],
        out_specs=[VMEM] * 4,
        out_shape=[out, out, back, back],
        compiler_params=PARAMS,
        name="prepare_transfer",
    )(vals)


def restrict_pairs(prol_col, pairs, high_ref, low_ref, total):
    n = pairs.shape[0]
    high, low = two_parts(pairs)
    left = jnp.concatenate([high, low], 1).astype(BF16).reshape(16 * n, 256)
    total[...] = jnp.zeros_like(total)
    for g in range(n // 8):
        out = row_products(left[128 * g : 128 * g + 128], high_ref, low_ref, g)
        for r in range(8):
            c = prol_col[0, 8 * g + r]
            total[c] = total[c] + (out[16 * r : 16 * r + 8] + out[16 * r + 8 : 16 * r + 16])
    first, last = corners()
    whole = jnp.where(first | last, total[...], 0.0)
    whole = whole + other_lane(whole)
    return whole + other_row(whole)


def to_pairs(vector):
    rows = masked_rows(vector)
    n = rows.shape[0]
    lane = lax.broadcasted_iota(jnp.int32, (128, 256), 0)
    pair = lax.broadcasted_iota(jnp.int32, (128, 256), 1) // 8
    gather = ((lane % 64) == 2 * pair + lane // 64).astype(F32).astype(BF16)
    both = jnp.dot(rows.reshape(16 * n, 128), gather, preferred_element_type=F32).reshape(n, 16, 256)
    whole = both[:, :8] + both[:, 8:]
    lane8 = own_lane(256)
    return jnp.concatenate([jnp.where(lane8 == i % 8, whole[i], 0.0)[None] for i in range(n)], 0)


def pairs_kernel(vector, pairs):
    pairs[...] = to_pairs(vector[...])


def by_slot(col, i, k):
    return col[k - 1, i]


def by_row(col, i, k):
    return col[i, k - 1]


def smooth_kernel(step, count, at, col, own, outer, partner, high, low, resid, total, new_resid, new_d, new_total, window, left):
    fill_window(window, own, partner, outer)
    product = operator(functools.partial(at, col), 7, window, left, high, low, count)
    r = resid[...] - product
    d = step[0] * own[...] + step[1] * r
    new_resid[...] = r
    new_d[...] = d
    new_total[...] = total[...] + d


def total_kernel(step, count, at, col, own, outer, partner, high, low, resid, total, new_total, window, left):
    fill_window(window, own, partner, outer)
    product = operator(functools.partial(at, col), 7, window, left, high, low, count)
    new_total[...] = total[...] + step[0] * own[...] + step[1] * (resid[...] - product)


def restrict_kernel(
    count, col, prol_col, own, outer, partner, high, low, resid, back_high, back_low,
    pairs, to_partner, to_own, to_outer, window, left, sums,
):
    fill_window(window, own, partner, outer)
    product = operator_pairs(functools.partial(by_slot, col), 7, window, left, high, low, count)
    pairs[...] = product
    whole = restrict_pairs(prol_col, resid[...] - product, back_high, back_low, sums)
    m = whole.shape[0] // 3
    to_partner[...] = pack_quarters(whole[:m])
    to_own[...] = pack_quarters(whole[m : 2 * m])
    to_outer[...] = pack_quarters(whole[2 * m :])


def second_kernel(pairs, resid, second):
    second[...] = resid[...] - from_pairs(pairs[...])


def sum_kernel(own, outer, partner, total):
    total[...] = own[...] + outer[...] + partner[...]


def prolong_kernel(prol_col, own, outer, partner, high, low, total, spread, new_total, window, left):
    fill_window(window, own, partner, outer)
    product = operator(lambda i, k: prol_col[0, i], 1, window, left, high, low, None)
    spread[...] = product
    new_total[...] = total[...] + product


def resid_kernel(count, col, own, outer, partner, high, low, resid, total, new_resid, new_total, window, left):
    fill_window(window, own, partner, outer)
    product = operator(functools.partial(by_slot, col), 7, window, left, high, low, count)
    r = resid[...] - product
    new_resid[...] = r
    new_total[...] = total[...] + r


def last_kernel(count, col, own, outer, partner, high, low, resid, total, *rest):
    *others, solution_out, resid_out, window, left = rest
    del others
    fill_window(window, own, partner, outer)
    product = operator(functools.partial(by_slot, col), 7, window, left, high, low, count)
    unpack_to(resid_out, resid[...] - product)
    unpack_to(solution_out, total[...])


def keep_others(*refs):
    other_solution, other_resid, solution_out, resid_out = refs[-6:-2]
    solution_out[...] = other_solution[...]
    resid_out[...] = other_resid[...]


def operator_scratch(window_blocks, rows, slots):
    return [pltpu.VMEM((window_blocks, 16, 128), BF16), pltpu.VMEM((16 * rows, 128 * slots), BF16)]


class Chain:
    last = None

    def __init__(self, rank, parity):
        self.rank = rank
        self.parity = parity

    def call(self, kernel, name, scalars, vectors, outs, scratch, otherwise=None):
        def guarded(rank, previous, *refs):
            del previous

            @pl.when((rank[0] & 1) == self.parity)
            def _():
                kernel(*refs)

            if otherwise is not None:

                @pl.when((rank[0] & 1) != self.parity)
                def _():
                    otherwise(*refs)

        if Chain.last is None:
            Chain.last = vectors[0]
        results = pl.pallas_call(
            guarded,
            in_specs=[SMEM, pl.BlockSpec(memory_space=pl.ANY)] + [SMEM] * len(scalars) + [VMEM] * len(vectors),
            out_specs=[VMEM] * len(outs),
            out_shape=[
                out if isinstance(out, jax.ShapeDtypeStruct)
                else pltpu.VMEM(out if isinstance(out, tuple) else (out // 4, 8, 128), F32)
                for out in outs
            ],
            scratch_shapes=scratch,
            compiler_params=PARAMS,
            name=name,
        )(self.rank, Chain.last, *scalars, *vectors)
        Chain.last = results[0]
        return results


def turns(steps):
    done = [0, 0]
    which, run = 0, 1
    while min(done) < steps:
        for _ in range(run):
            if done[which] < steps:
                yield which
                done[which] += 1
        which, run = 1 - which, 2


def packed_tiles(vector):
    q = vector.shape[0] // 4
    top = jnp.concatenate([vector[:q], vector[2 * q : 3 * q]], -1)
    bottom = jnp.concatenate([vector[3 * q :], vector[q : 2 * q]], -1)
    return jnp.concatenate([top, bottom], 1)


def pack_kernel(rank, *refs):
    del rank
    for vector, packed in zip(refs[: len(refs) // 2], refs[len(refs) // 2 :]):
        packed[...] = packed_tiles(vector)


def pack(rank, *vectors):
    blocks, sides, width = vectors[0].shape
    shape = pltpu.VMEM((blocks // 4, 2 * sides, 2 * width), F32)
    return pl.pallas_call(
        pack_kernel,
        in_specs=[SMEM] + [VMEM] * len(vectors),
        out_specs=[VMEM] * len(vectors),
        out_shape=[shape] * len(vectors),
        compiler_params=PARAMS,
        name="pack",
    )(rank, *vectors)


def unpack_to(out, packed):
    q = packed.shape[0]
    out[:q] = packed[:, :4, :64]
    out[q : 2 * q] = packed[:, 4:, 64:]
    out[2 * q : 3 * q] = packed[:, :4, 64:]
    out[3 * q :] = packed[:, 4:, :64]


def begin_kernel(n, m, slots, rank, vals, *refs):
    cols, (high_ref, low_ref), places = refs[:3], refs[3:5], refs[5:8]
    held, arrived, *small = refs[8:]
    here, there, sems = small[:3], small[3:6], small[6]
    come = [pltpu.make_async_copy(cols[i], here[i], sems.at[i]) for i in range(3)]
    leave = [pltpu.make_async_copy(there[i], places[i], sems.at[3 + i]) for i in range(3)]

    def indices():
        for i, per_device in enumerate((n, m, m)):
            come[i].wait()
            block = here[i][...]
            place = block - rank[0] * per_device
            inner = block - (rank[0] ^ 1) * per_device
            outer = lax.rem(block, per_device) + 2 * per_device
            own = (place >= 0) & (place < per_device)
            beside = (inner >= 0) & (inner < per_device)
            there[i][...] = jnp.where(own, place + per_device, jnp.where(beside, inner, outer))
            leave[i].start()

    for copy in come:
        copy.start()
    split_groups(n // 8, slots, vals, high_ref, low_ref, held, arrived, indices)
    for copy in leave:
        copy.wait()


def begin(rank, vals, m, *cols):
    n, slots, width = vals.shape
    shape = pltpu.VMEM((n // 8, 128 * slots, 256), BF16)
    hbm = pl.BlockSpec(memory_space=pltpu.HBM)
    return pl.pallas_call(
        functools.partial(begin_kernel, n, m, slots),
        in_specs=[SMEM] + [hbm] * 4,
        out_specs=[VMEM] * 2 + [SMEM] * 3,
        out_shape=[shape, shape] + [pltpu.SMEM(c.shape, jnp.int32) for c in cols],
        scratch_shapes=[
            pltpu.VMEM((n // 8, slots, 8, width), F32),
            pltpu.SemaphoreType.DMA((n // 8,)),
            *[pltpu.VMEM(c.shape, jnp.int32) for c in cols * 2],
            pltpu.SemaphoreType.DMA((6,)),
        ],
        compiler_params=STREAM_PARAMS,
        name="begin",
    )(rank, vals.transpose(1, 0, 2), *cols)


def body(right_side, fine_vals, fine_cols, prol_vals, prol_cols, coarse_vals, coarse_cols):
    devices = lax.axis_size("fine")
    rank = jnp.reshape(lax.axis_index("fine"), (1,))
    n = right_side.shape[0]
    m = coarse_vals.shape[0]

    up = [(i, (i + 1) % devices) for i in range(devices)]
    down = [((i + 1) % devices, i) for i in range(devices)]
    inside = [(i, i ^ 1) for i in range(devices)]
    across = [(i, (i + 1 if i % 2 else i - 1) % devices) for i in range(devices)]

    from_outer = lax.ppermute(right_side, "fine", across)
    from_partner = lax.ppermute(right_side, "fine", inside)
    high, low, fine_at, prol_at, coarse_at = begin(
        rank, fine_vals, m, fine_cols.T, prol_cols.reshape(1, n), coarse_cols
    )
    coarse_high, coarse_low = prepare(rank, coarse_vals)
    prol_high, prol_low, back_high, back_low = prepare_transfer(prol_vals)

    from_outer, from_partner, first = pack(rank, from_outer, from_partner, right_side)

    def steps(chain):
        def fine(kernel, name, d, more, outs, scalars=(), scratch=(), after=()):
            partner, outer = yield d, d
            vectors = (d, outer, partner, high, low, *more, *after)
            return chain.call(kernel, name, (fine_at, *scalars), vectors, outs, operator_scratch(3 * n, n, 7) + list(scratch))

        def fine_smooth(d, resid, total, step):
            kernel = functools.partial(smooth_kernel, step, n, by_slot)
            return (yield from fine(kernel, "fine_smooth", d, (resid, total), [n, n, n]))

        def fine_resid(d, resid, total):
            kernel = functools.partial(resid_kernel, n)
            return (yield from fine(kernel, "fine_resid", d, (resid, total), [n, n]))

        def coarse(kernel, name, d, resid, total, step, outs):
            partner, outer = yield d, d
            vectors = (d, outer, partner, coarse_high, coarse_low, resid, total)
            kernel = functools.partial(kernel, step, m, by_row)
            return chain.call(kernel, name, (coarse_at,), vectors, outs, operator_scratch(3 * m, m, 7))

        def cycle(resid, total):
            resid, d, total = yield from fine_smooth(resid, resid, total, STEP1)
            resid, d, total = yield from fine_smooth(d, resid, total, STEP2)
            sums = [pltpu.VMEM((3 * m, 8, 128), F32)]
            (resid_pairs,) = chain.call(pairs_kernel, "resid_pairs", (), (resid,), [(n, 8, 256)], [])
            pairs, to_partner, to_own, to_outer = yield from fine(
                functools.partial(restrict_kernel, n), "fine_restrict", d, (resid_pairs,), [(n, 8, 256), m, m, m],
                scalars=(prol_at,), scratch=sums, after=(back_high, back_low),
            )
            (second,) = chain.call(second_kernel, "fine_second", (), (pairs, resid), [n], [])
            partner, outer = yield to_partner, to_outer
            (right,) = chain.call(sum_kernel, "coarse_sum", (), (to_own, outer, partner), [m], [])
            resid, d, fix = yield from coarse(smooth_kernel, "coarse_smooth", right, right, right, STEP1, [m, m, m])
            (fix,) = yield from coarse(total_kernel, "coarse_total", d, resid, fix, STEP2, [m])
            partner, outer = yield fix, fix
            spread, total = chain.call(
                prolong_kernel, "prolong", (prol_at,),
                (fix, outer, partner, prol_high, prol_low, total), [n, n], operator_scratch(3 * m, n, 1),
            )
            resid, total = yield from fine_resid(spread, second, total)
            resid, d, total = yield from fine_smooth(resid, resid, total, STEP1)
            resid, d, total = yield from fine_smooth(d, resid, total, STEP2)
            return d, resid, total

        d, resid, total = yield from cycle(first, first)
        resid, total = yield from fine_resid(d, resid, total)
        d, resid, total = yield from cycle(resid, total)
        partner, outer = yield d, d
        vectors = (d, outer, partner, high, low, resid, total, *finished)
        finished[:] = chain.call(
            functools.partial(last_kernel, n), "fine_last", (fine_at,), vectors,
            [jax.ShapeDtypeStruct(right_side.shape, F32)] * 2, operator_scratch(3 * n, n, 7), keep_others if finished else None,
        )

    finished = []
    Chain.last = None
    chains = [steps(Chain(rank, 1)), steps(Chain(rank, 0))]
    for chain in chains:
        next(chain)
    inbox = [[(from_partner, from_outer)], [(from_partner, from_outer)]]
    for which in turns(22):
        try:
            to_partner, to_outer = chains[which].send(inbox[which].pop(0))
        except StopIteration:
            continue
        partner = lax.ppermute(to_partner, "fine", inside)
        outer = lax.ppermute(to_outer, "fine", (up, down)[which])
        inbox[1 - which].append((partner, outer))
    return tuple(finished)


def solution(mesh):
    in_specs = (
        P("fine", None, None),
        P("fine", None, None),
        P("fine", None),
        P("fine", None),
        P("fine"),
        P("fine", None, None),
        P("fine", None),
    )
    out_specs = (P("fine", None, None), P("fine", None, None))
    return jax.shard_map(body, mesh=mesh, in_specs=in_specs, out_specs=out_specs, check_vma=False)
```

```python
import functools

import jax
import jax.numpy as jnp
from jax import lax
from jax.experimental import pallas as pl
from jax.experimental.pallas import tpu as pltpu
from jax.sharding import PartitionSpec as P

THETA = 1.0
DELTA = 0.75
SIGMA = THETA / DELTA
RHO0 = 1.0 / SIGMA
RHO1 = 1.0 / (2.0 * SIGMA - RHO0)
RHO2 = 1.0 / (2.0 * SIGMA - RHO1)
STEP1 = (RHO1 * RHO0, 2.0 * RHO1 / DELTA)
STEP2 = (RHO2 * RHO1, 2.0 * RHO2 / DELTA)

F32 = jnp.float32
BF16 = jnp.bfloat16
VMEM = pl.BlockSpec(memory_space=pltpu.VMEM)
SMEM = pl.BlockSpec(memory_space=pltpu.SMEM)
PARAMS = pltpu.CompilerParams(vmem_limit_bytes=16 * 2**20)
STREAM_PARAMS = pltpu.CompilerParams(vmem_limit_bytes=48 * 2**20)


def halves():
    row = lax.broadcasted_iota(jnp.int32, (1, 8, 128), 1)
    lane = lax.broadcasted_iota(jnp.int32, (1, 8, 128), 2)
    return row < 4, lane < 64


def corners():
    top, front = halves()
    return top & front, jnp.logical_not(top | front)


def other_row(x):
    return pltpu.roll(x, 4, 1)


def other_lane(x):
    return pltpu.roll(x, 64, 2)


def pack_quarters(whole):
    top, front = halves()
    q = whole.shape[0] // 4
    first = jnp.where(front, whole[:q], whole[2 * q : 3 * q])
    return jnp.where(top, first, jnp.where(front, whole[3 * q :], whole[q : 2 * q]))


def two_parts(x):
    high = x.astype(BF16).astype(F32)
    return high, x - high


def masked_rows(packed):
    first, last = corners()
    lanes = other_lane(packed)
    rows = other_row(packed)
    both = other_row(lanes)
    blocks = [
        jnp.where(first, packed, jnp.where(last, both, 0.0)),
        jnp.where(last, packed, jnp.where(first, both, 0.0)),
        jnp.where(first, lanes, jnp.where(last, rows, 0.0)),
        jnp.where(last, lanes, jnp.where(first, rows, 0.0)),
    ]
    high, low = two_parts(jnp.concatenate(blocks, 0))
    return jnp.concatenate([high, low], 1).astype(BF16)


def own_lane(width):
    return lax.broadcasted_iota(jnp.int32, (8, width), 1) % 8


def from_pairs(rows):
    n = rows.shape[0]
    pair = lax.broadcasted_iota(jnp.int32, (256, 256), 0) // 8
    lane = lax.broadcasted_iota(jnp.int32, (256, 256), 1)
    spread = ((lane % 64) == 2 * pair + lane // 128).astype(F32).astype(BF16)
    high, low = two_parts(rows.reshape(n * 8, 256))
    both = jnp.concatenate([high, low], 0).astype(BF16)
    y = jnp.dot(both, spread, preferred_element_type=F32)
    y = (y[: n * 8] + y[n * 8 :]).reshape(n, 8, 256)
    y = jnp.where(halves()[0], y[:, :, :128], y[:, :, 128:])
    return pack_quarters(y + other_row(y))


def row_products(left, high_ref, low_ref, group):
    out = jnp.dot(left, high_ref[group], preferred_element_type=F32)
    return out + jnp.dot(left, low_ref[group], preferred_element_type=F32)


def pick_rows(out):
    picked = []
    lane = own_lane(out.shape[1])
    for r in range(8):
        both = out[16 * r : 16 * r + 8] + out[16 * r + 8 : 16 * r + 16]
        picked.append(jnp.where(lane == r, both, 0.0)[None])
    return picked


def fill_window(window, own, partner, outer):
    n = 4 * own.shape[0]
    window[0:n] = masked_rows(partner[...])
    window[n : 2 * n] = masked_rows(own[...])
    window[2 * n : 3 * n] = masked_rows(outer[...])


def operator_pairs(col, slots, window, left, high_ref, low_ref, first):
    picked = []
    for g in range(high_ref.shape[0]):
        for i in range(8 * g, 8 * g + 8):
            for k in range(slots):
                at = first + i if (first is not None and k == 0) else col(i, k)
                left[16 * i : 16 * i + 16, 128 * k : 128 * k + 128] = window[at]
        out = row_products(left[128 * g : 128 * g + 128, 0 : 128 * slots], high_ref, low_ref, g)
        picked += pick_rows(out)
    return jnp.concatenate(picked, 0)


def operator(*args):
    return from_pairs(operator_pairs(*args))


def split_groups(groups, slots, vals, high_ref, low_ref, held, arrived, meanwhile=None):
    def fetch(g):
        return pltpu.make_async_copy(vals.at[:, pl.ds(8 * g, 8), :], held.at[g], arrived.at[g])

    for g in range(min(3, groups)):
        fetch(g).start()
    if meanwhile is not None:
        meanwhile()
    for g in range(groups):
        if g + 3 < groups:
            fetch(g + 3).start()
        fetch(g).wait()
        for k in range(slots):
            block = jnp.concatenate([held[g, k, :, 128 * t : 128 * t + 128] for t in range(32)], 0).T
            high, low = two_parts(block)
            high_ref[g, 128 * k : 128 * k + 128, :] = high.astype(BF16)
            low_ref[g, 128 * k : 128 * k + 128, :] = low.astype(BF16)


def prepare_kernel(groups, slots, rank, *refs):
    del rank
    split_groups(groups, slots, *refs)


def prepare(rank, vals):
    rows, slots, width = vals.shape
    shape = pltpu.VMEM((rows // 8, 128 * slots, 256), BF16)
    return pl.pallas_call(
        functools.partial(prepare_kernel, rows // 8, slots),
        in_specs=[SMEM, pl.BlockSpec(memory_space=pltpu.HBM)],
        out_specs=[VMEM, VMEM],
        out_shape=[shape, shape],
        scratch_shapes=[pltpu.VMEM((rows // 8, slots, 8, width), F32), pltpu.SemaphoreType.DMA((rows // 8,))],
        compiler_params=PARAMS,
        name="prepare",
    )(rank, vals.transpose(1, 0, 2))


def prepare_transfer_kernel(vals, high_ref, low_ref, high_back_ref, low_back_ref):
    g = pl.program_id(0)
    block = jnp.concatenate([vals[:, 128 * t : 128 * t + 128] for t in range(32)], 0)
    high, low = two_parts(block)
    high_back_ref[g] = high.astype(BF16)
    low_back_ref[g] = low.astype(BF16)
    high, low = two_parts(block.T)
    high_ref[g] = high.astype(BF16)
    low_ref[g] = low.astype(BF16)


def prepare_transfer(vals):
    rows, width = vals.shape
    out = pltpu.VMEM((rows // 8, 128, 256), BF16)
    back = pltpu.VMEM((rows // 8, 256, 128), BF16)
    return pl.pallas_call(
        prepare_transfer_kernel,
        grid=(rows // 8,),
        in_specs=[pl.BlockSpec((8, width), lambda g: (g, 0))],
        out_specs=[VMEM] * 4,
        out_shape=[out, out, back, back],
        compiler_params=PARAMS,
        name="prepare_transfer",
    )(vals)


def restrict_pairs(prol_col, pairs, high_ref, low_ref, total):
    n = pairs.shape[0]
    high, low = two_parts(pairs)
    left = jnp.concatenate([high, low], 1).astype(BF16).reshape(16 * n, 256)
    total[...] = jnp.zeros_like(total)
    for g in range(n // 8):
        out = row_products(left[128 * g : 128 * g + 128], high_ref, low_ref, g)
        for r in range(8):
            c = prol_col[0, 8 * g + r]
            total[c] = total[c] + (out[16 * r : 16 * r + 8] + out[16 * r + 8 : 16 * r + 16])
    first, last = corners()
    whole = jnp.where(first | last, total[...], 0.0)
    whole = whole + other_lane(whole)
    return whole + other_row(whole)


def to_pairs(vector):
    rows = masked_rows(vector)
    n = rows.shape[0]
    lane = lax.broadcasted_iota(jnp.int32, (128, 256), 0)
    pair = lax.broadcasted_iota(jnp.int32, (128, 256), 1) // 8
    gather = ((lane % 64) == 2 * pair + lane // 64).astype(F32).astype(BF16)
    both = jnp.dot(rows.reshape(16 * n, 128), gather, preferred_element_type=F32).reshape(n, 16, 256)
    whole = both[:, :8] + both[:, 8:]
    lane8 = own_lane(256)
    return jnp.concatenate([jnp.where(lane8 == i % 8, whole[i], 0.0)[None] for i in range(n)], 0)


def pairs_kernel(vector, pairs):
    pairs[...] = to_pairs(vector[...])


def by_slot(col, i, k):
    return col[k - 1, i]


def by_row(col, i, k):
    return col[i, k - 1]


def smooth_kernel(step, count, at, col, own, outer, partner, high, low, resid, total, new_resid, new_d, new_total, window, left):
    fill_window(window, own, partner, outer)
    product = operator(functools.partial(at, col), 7, window, left, high, low, count)
    r = resid[...] - product
    d = step[0] * own[...] + step[1] * r
    new_resid[...] = r
    new_d[...] = d
    new_total[...] = total[...] + d


def total_kernel(step, count, at, col, own, outer, partner, high, low, resid, total, new_total, window, left):
    fill_window(window, own, partner, outer)
    product = operator(functools.partial(at, col), 7, window, left, high, low, count)
    new_total[...] = total[...] + step[0] * own[...] + step[1] * (resid[...] - product)


def restrict_kernel(
    count, col, prol_col, own, outer, partner, high, low, resid, back_high, back_low,
    pairs, to_partner, to_own, to_outer, window, left, sums,
):
    fill_window(window, own, partner, outer)
    product = operator_pairs(functools.partial(by_slot, col), 7, window, left, high, low, count)
    pairs[...] = product
    whole = restrict_pairs(prol_col, resid[...] - product, back_high, back_low, sums)
    m = whole.shape[0] // 3
    to_partner[...] = pack_quarters(whole[:m])
    to_own[...] = pack_quarters(whole[m : 2 * m])
    to_outer[...] = pack_quarters(whole[2 * m :])


def second_kernel(pairs, resid, second):
    second[...] = resid[...] - from_pairs(pairs[...])


def sum_kernel(own, outer, partner, total):
    total[...] = own[...] + outer[...] + partner[...]


def prolong_kernel(prol_col, own, outer, partner, high, low, total, spread, new_total, window, left):
    fill_window(window, own, partner, outer)
    product = operator(lambda i, k: prol_col[0, i], 1, window, left, high, low, None)
    spread[...] = product
    new_total[...] = total[...] + product


def resid_kernel(count, col, own, outer, partner, high, low, resid, total, new_resid, new_total, window, left):
    fill_window(window, own, partner, outer)
    product = operator(functools.partial(by_slot, col), 7, window, left, high, low, count)
    r = resid[...] - product
    new_resid[...] = r
    new_total[...] = total[...] + r


def solution_kernel(total, *rest):
    unpack_to(rest[-1], total[...])


def last_kernel(count, col, own, outer, partner, high, low, resid, *rest):
    *others, out, window, left = rest
    del others
    fill_window(window, own, outer=outer, partner=partner)
    product = operator(functools.partial(by_slot, col), 7, window, left, high, low, count)
    unpack_to(out, resid[...] - product)


def keep_solution(total, other, out):
    del total
    out[...] = other[...]


def keep_resid(*refs):
    other, out = refs[-4:-2]
    out[...] = other[...]


def operator_scratch(window_blocks, rows, slots):
    return [pltpu.VMEM((window_blocks, 16, 128), BF16), pltpu.VMEM((16 * rows, 128 * slots), BF16)]


class Chain:
    last = None

    def __init__(self, rank, parity):
        self.rank = rank
        self.parity = parity

    def call(self, kernel, name, scalars, vectors, outs, scratch, otherwise=None):
        def guarded(rank, previous, *refs):
            del previous

            @pl.when((rank[0] & 1) == self.parity)
            def _():
                kernel(*refs)

            if otherwise is not None:

                @pl.when((rank[0] & 1) != self.parity)
                def _():
                    otherwise(*refs)

        if Chain.last is None:
            Chain.last = vectors[0]
        results = pl.pallas_call(
            guarded,
            in_specs=[SMEM, pl.BlockSpec(memory_space=pl.ANY)] + [SMEM] * len(scalars) + [VMEM] * len(vectors),
            out_specs=[VMEM] * len(outs),
            out_shape=[
                out if isinstance(out, jax.ShapeDtypeStruct)
                else pltpu.VMEM(out if isinstance(out, tuple) else (out // 4, 8, 128), F32)
                for out in outs
            ],
            scratch_shapes=scratch,
            compiler_params=PARAMS,
            name=name,
        )(self.rank, Chain.last, *scalars, *vectors)
        Chain.last = results[0]
        return results


def turns(steps):
    done = [0, 0]
    which, run = 0, 1
    while min(done) < steps:
        for _ in range(run):
            if done[which] < steps:
                yield which
                done[which] += 1
        which, run = 1 - which, 2


def packed_tiles(vector):
    q = vector.shape[0] // 4
    top = jnp.concatenate([vector[:q], vector[2 * q : 3 * q]], -1)
    bottom = jnp.concatenate([vector[3 * q :], vector[q : 2 * q]], -1)
    return jnp.concatenate([top, bottom], 1)


def pack_kernel(rank, *refs):
    del rank
    for vector, packed in zip(refs[: len(refs) // 2], refs[len(refs) // 2 :]):
        packed[...] = packed_tiles(vector)


def pack(rank, *vectors):
    blocks, sides, width = vectors[0].shape
    shape = pltpu.VMEM((blocks // 4, 2 * sides, 2 * width), F32)
    return pl.pallas_call(
        pack_kernel,
        in_specs=[SMEM] + [VMEM] * len(vectors),
        out_specs=[VMEM] * len(vectors),
        out_shape=[shape] * len(vectors),
        compiler_params=PARAMS,
        name="pack",
    )(rank, *vectors)


def unpack_to(out, packed):
    q = packed.shape[0]
    out[:q] = packed[:, :4, :64]
    out[q : 2 * q] = packed[:, 4:, 64:]
    out[2 * q : 3 * q] = packed[:, :4, 64:]
    out[3 * q :] = packed[:, 4:, :64]


def begin_kernel(n, m, slots, rank, vals, *refs):
    cols, (high_ref, low_ref), places = refs[:3], refs[3:5], refs[5:8]
    held, arrived, *small = refs[8:]
    here, there, sems = small[:3], small[3:6], small[6]
    come = [pltpu.make_async_copy(cols[i], here[i], sems.at[i]) for i in range(3)]
    leave = [pltpu.make_async_copy(there[i], places[i], sems.at[3 + i]) for i in range(3)]

    def indices():
        for i, per_device in enumerate((n, m, m)):
            come[i].wait()
            block = here[i][...]
            place = block - rank[0] * per_device
            inner = block - (rank[0] ^ 1) * per_device
            outer = lax.rem(block, per_device) + 2 * per_device
            own = (place >= 0) & (place < per_device)
            beside = (inner >= 0) & (inner < per_device)
            there[i][...] = jnp.where(own, place + per_device, jnp.where(beside, inner, outer))
            leave[i].start()

    for copy in come:
        copy.start()
    split_groups(n // 8, slots, vals, high_ref, low_ref, held, arrived, indices)
    for copy in leave:
        copy.wait()


def begin(rank, vals, m, *cols):
    n, slots, width = vals.shape
    shape = pltpu.VMEM((n // 8, 128 * slots, 256), BF16)
    hbm = pl.BlockSpec(memory_space=pltpu.HBM)
    return pl.pallas_call(
        functools.partial(begin_kernel, n, m, slots),
        in_specs=[SMEM] + [hbm] * 4,
        out_specs=[VMEM] * 2 + [SMEM] * 3,
        out_shape=[shape, shape] + [pltpu.SMEM(c.shape, jnp.int32) for c in cols],
        scratch_shapes=[
            pltpu.VMEM((n // 8, slots, 8, width), F32),
            pltpu.SemaphoreType.DMA((n // 8,)),
            *[pltpu.VMEM(c.shape, jnp.int32) for c in cols * 2],
            pltpu.SemaphoreType.DMA((6,)),
        ],
        compiler_params=STREAM_PARAMS,
        name="begin",
    )(rank, vals.transpose(1, 0, 2), *cols)


def body(right_side, fine_vals, fine_cols, prol_vals, prol_cols, coarse_vals, coarse_cols):
    devices = lax.axis_size("fine")
    rank = jnp.reshape(lax.axis_index("fine"), (1,))
    n = right_side.shape[0]
    m = coarse_vals.shape[0]

    up = [(i, (i + 1) % devices) for i in range(devices)]
    down = [((i + 1) % devices, i) for i in range(devices)]
    inside = [(i, i ^ 1) for i in range(devices)]
    across = [(i, (i + 1 if i % 2 else i - 1) % devices) for i in range(devices)]

    from_outer = lax.ppermute(right_side, "fine", across)
    from_partner = lax.ppermute(right_side, "fine", inside)
    high, low, fine_at, prol_at, coarse_at = begin(
        rank, fine_vals, m, fine_cols.T, prol_cols.reshape(1, n), coarse_cols
    )
    coarse_high, coarse_low = prepare(rank, coarse_vals)
    prol_high, prol_low, back_high, back_low = prepare_transfer(prol_vals)

    from_outer, from_partner, first = pack(rank, from_outer, from_partner, right_side)

    def steps(chain):
        def fine(kernel, name, d, more, outs, scalars=(), scratch=(), after=()):
            partner, outer = yield d, d
            vectors = (d, outer, partner, high, low, *more, *after)
            return chain.call(kernel, name, (fine_at, *scalars), vectors, outs, operator_scratch(3 * n, n, 7) + list(scratch))

        def fine_smooth(d, resid, total, step):
            kernel = functools.partial(smooth_kernel, step, n, by_slot)
            return (yield from fine(kernel, "fine_smooth", d, (resid, total), [n, n, n]))

        def fine_resid(d, resid, total):
            kernel = functools.partial(resid_kernel, n)
            return (yield from fine(kernel, "fine_resid", d, (resid, total), [n, n]))

        def coarse(kernel, name, d, resid, total, step, outs):
            partner, outer = yield d, d
            vectors = (d, outer, partner, coarse_high, coarse_low, resid, total)
            kernel = functools.partial(kernel, step, m, by_row)
            return chain.call(kernel, name, (coarse_at,), vectors, outs, operator_scratch(3 * m, m, 7))

        def cycle(resid, total):
            resid, d, total = yield from fine_smooth(resid, resid, total, STEP1)
            resid, d, total = yield from fine_smooth(d, resid, total, STEP2)
            sums = [pltpu.VMEM((3 * m, 8, 128), F32)]
            (resid_pairs,) = chain.call(pairs_kernel, "resid_pairs", (), (resid,), [(n, 8, 256)], [])
            pairs, to_partner, to_own, to_outer = yield from fine(
                functools.partial(restrict_kernel, n), "fine_restrict", d, (resid_pairs,), [(n, 8, 256), m, m, m],
                scalars=(prol_at,), scratch=sums, after=(back_high, back_low),
            )
            (second,) = chain.call(second_kernel, "fine_second", (), (pairs, resid), [n], [])
            partner, outer = yield to_partner, to_outer
            (right,) = chain.call(sum_kernel, "coarse_sum", (), (to_own, outer, partner), [m], [])
            resid, d, fix = yield from coarse(smooth_kernel, "coarse_smooth", right, right, right, STEP1, [m, m, m])
            (fix,) = yield from coarse(total_kernel, "coarse_total", d, resid, fix, STEP2, [m])
            partner, outer = yield fix, fix
            spread, total = chain.call(
                prolong_kernel, "prolong", (prol_at,),
                (fix, outer, partner, prol_high, prol_low, total), [n, n], operator_scratch(3 * m, n, 1),
            )
            resid, total = yield from fine_resid(spread, second, total)
            resid, d, total = yield from fine_smooth(resid, resid, total, STEP1)
            resid, d, total = yield from fine_smooth(d, resid, total, STEP2)
            return d, resid, total

        d, resid, total = yield from cycle(first, first)
        resid, total = yield from fine_resid(d, resid, total)
        d, resid, total = yield from cycle(resid, total)
        written[:] = chain.call(
            solution_kernel, "solution", (), (total, *written),
            [jax.ShapeDtypeStruct(right_side.shape, F32) if written else right_side.shape], [],
            keep_solution if written else None,
        )
        partner, outer = yield d, d
        vectors = (d, outer, partner, high, low, resid, *finished)
        finished[:] = chain.call(
            functools.partial(last_kernel, n), "fine_last", (fine_at,), vectors,
            [jax.ShapeDtypeStruct(right_side.shape, F32)], operator_scratch(3 * n, n, 7), keep_resid if finished else None,
        )

    written, finished = [], []
    Chain.last = None
    chains = [steps(Chain(rank, 1)), steps(Chain(rank, 0))]
    for chain in chains:
        next(chain)
    inbox = [[(from_partner, from_outer)], [(from_partner, from_outer)]]
    for which in turns(22):
        try:
            to_partner, to_outer = chains[which].send(inbox[which].pop(0))
        except StopIteration:
            continue
        partner = lax.ppermute(to_partner, "fine", inside)
        outer = lax.ppermute(to_outer, "fine", (up, down)[which])
        inbox[1 - which].append((partner, outer))
    return written[0], finished[0]


def solution(mesh):
    in_specs = (
        P("fine", None, None),
        P("fine", None, None),
        P("fine", None),
        P("fine", None),
        P("fine"),
        P("fine", None, None),
        P("fine", None),
    )
    out_specs = (P("fine", None, None), P("fine", None, None))
    return jax.shard_map(body, mesh=mesh, in_specs=in_specs, out_specs=out_specs, check_vma=False)
```

```python
import functools

import jax
import jax.numpy as jnp
from jax import lax
from jax.experimental import pallas as pl
from jax.experimental.pallas import tpu as pltpu
from jax.sharding import PartitionSpec as P

THETA = 1.0
DELTA = 0.75
SIGMA = THETA / DELTA
RHO0 = 1.0 / SIGMA
RHO1 = 1.0 / (2.0 * SIGMA - RHO0)
RHO2 = 1.0 / (2.0 * SIGMA - RHO1)
STEP1 = (RHO1 * RHO0, 2.0 * RHO1 / DELTA)
STEP2 = (RHO2 * RHO1, 2.0 * RHO2 / DELTA)

F32 = jnp.float32
BF16 = jnp.bfloat16
VMEM = pl.BlockSpec(memory_space=pltpu.VMEM)
SMEM = pl.BlockSpec(memory_space=pltpu.SMEM)
PARAMS = pltpu.CompilerParams(vmem_limit_bytes=16 * 2**20)
STREAM_PARAMS = pltpu.CompilerParams(vmem_limit_bytes=48 * 2**20)


def halves():
    row = lax.broadcasted_iota(jnp.int32, (1, 8, 128), 1)
    lane = lax.broadcasted_iota(jnp.int32, (1, 8, 128), 2)
    return row < 4, lane < 64


def corners():
    top, front = halves()
    return top & front, jnp.logical_not(top | front)


def other_row(x):
    return pltpu.roll(x, 4, 1)


def other_lane(x):
    return pltpu.roll(x, 64, 2)


def pack_quarters(whole):
    top, front = halves()
    q = whole.shape[0] // 4
    first = jnp.where(front, whole[:q], whole[2 * q : 3 * q])
    return jnp.where(top, first, jnp.where(front, whole[3 * q :], whole[q : 2 * q]))


def two_parts(x):
    high = x.astype(BF16).astype(F32)
    return high, x - high


def masked_rows(packed):
    first, last = corners()
    lanes = other_lane(packed)
    rows = other_row(packed)
    both = other_row(lanes)
    blocks = [
        jnp.where(first, packed, jnp.where(last, both, 0.0)),
        jnp.where(last, packed, jnp.where(first, both, 0.0)),
        jnp.where(first, lanes, jnp.where(last, rows, 0.0)),
        jnp.where(last, lanes, jnp.where(first, rows, 0.0)),
    ]
    high, low = two_parts(jnp.concatenate(blocks, 0))
    return jnp.concatenate([high, low], 1).astype(BF16)


def own_lane(width):
    return lax.broadcasted_iota(jnp.int32, (8, width), 1) % 8


def from_pairs(rows):
    n = rows.shape[0]
    pair = lax.broadcasted_iota(jnp.int32, (256, 256), 0) // 8
    lane = lax.broadcasted_iota(jnp.int32, (256, 256), 1)
    spread = ((lane % 64) == 2 * pair + lane // 128).astype(F32).astype(BF16)
    high, low = two_parts(rows.reshape(n * 8, 256))
    both = jnp.concatenate([high, low], 0).astype(BF16)
    y = jnp.dot(both, spread, preferred_element_type=F32)
    y = (y[: n * 8] + y[n * 8 :]).reshape(n, 8, 256)
    y = jnp.where(halves()[0], y[:, :, :128], y[:, :, 128:])
    return pack_quarters(y + other_row(y))


def row_products(left, high_ref, low_ref, group):
    out = jnp.dot(left, high_ref[group], preferred_element_type=F32)
    return out + jnp.dot(left, low_ref[group], preferred_element_type=F32)


def pick_rows(out):
    picked = []
    lane = own_lane(out.shape[1])
    for r in range(8):
        both = out[16 * r : 16 * r + 8] + out[16 * r + 8 : 16 * r + 16]
        picked.append(jnp.where(lane == r, both, 0.0)[None])
    return picked


def fill_window(window, own, partner, outer):
    n = 4 * own.shape[0]
    window[0:n] = masked_rows(partner[...])
    window[n : 2 * n] = masked_rows(own[...])
    window[2 * n : 3 * n] = masked_rows(outer[...])


def operator_pairs(col, slots, window, left, high_ref, low_ref, first):
    picked = []
    for g in range(high_ref.shape[0]):
        for i in range(8 * g, 8 * g + 8):
            for k in range(slots):
                at = first + i if (first is not None and k == 0) else col(i, k)
                left[16 * i : 16 * i + 16, 128 * k : 128 * k + 128] = window[at]
        out = row_products(left[128 * g : 128 * g + 128, 0 : 128 * slots], high_ref, low_ref, g)
        picked += pick_rows(out)
    return jnp.concatenate(picked, 0)


def operator(*args):
    return from_pairs(operator_pairs(*args))


def split_groups(groups, slots, vals, high_ref, low_ref, held, arrived, meanwhile=None):
    def fetch(g):
        return pltpu.make_async_copy(vals.at[:, pl.ds(8 * g, 8), :], held.at[g], arrived.at[g])

    for g in range(min(3, groups)):
        fetch(g).start()
    if meanwhile is not None:
        meanwhile()
    for g in range(groups):
        if g + 3 < groups:
            fetch(g + 3).start()
        fetch(g).wait()
        for k in range(slots):
            block = jnp.concatenate([held[g, k, :, 128 * t : 128 * t + 128] for t in range(32)], 0).T
            high, low = two_parts(block)
            high_ref[g, 128 * k : 128 * k + 128, :] = high.astype(BF16)
            low_ref[g, 128 * k : 128 * k + 128, :] = low.astype(BF16)


def prepare_kernel(groups, slots, rank, *refs):
    del rank
    split_groups(groups, slots, *refs)


def prepare(rank, vals):
    rows, slots, width = vals.shape
    shape = pltpu.VMEM((rows // 8, 128 * slots, 256), BF16)
    return pl.pallas_call(
        functools.partial(prepare_kernel, rows // 8, slots),
        in_specs=[SMEM, pl.BlockSpec(memory_space=pltpu.HBM)],
        out_specs=[VMEM, VMEM],
        out_shape=[shape, shape],
        scratch_shapes=[pltpu.VMEM((rows // 8, slots, 8, width), F32), pltpu.SemaphoreType.DMA((rows // 8,))],
        compiler_params=PARAMS,
        name="prepare",
    )(rank, vals.transpose(1, 0, 2))


def prepare_transfer_kernel(vals, high_ref, low_ref, high_back_ref, low_back_ref):
    g = pl.program_id(0)
    block = jnp.concatenate([vals[:, 128 * t : 128 * t + 128] for t in range(32)], 0)
    high, low = two_parts(block)
    high_back_ref[g] = high.astype(BF16)
    low_back_ref[g] = low.astype(BF16)
    high, low = two_parts(block.T)
    high_ref[g] = high.astype(BF16)
    low_ref[g] = low.astype(BF16)


def prepare_transfer(vals):
    rows, width = vals.shape
    out = pltpu.VMEM((rows // 8, 128, 256), BF16)
    back = pltpu.VMEM((rows // 8, 256, 128), BF16)
    return pl.pallas_call(
        prepare_transfer_kernel,
        grid=(rows // 8,),
        in_specs=[pl.BlockSpec((8, width), lambda g: (g, 0))],
        out_specs=[VMEM] * 4,
        out_shape=[out, out, back, back],
        compiler_params=PARAMS,
        name="prepare_transfer",
    )(vals)


def restrict_pairs(prol_col, pairs, high_ref, low_ref, total):
    n = pairs.shape[0]
    high, low = two_parts(pairs)
    left = jnp.concatenate([high, low], 1).astype(BF16).reshape(16 * n, 256)
    total[...] = jnp.zeros_like(total)
    for g in range(n // 8):
        out = row_products(left[128 * g : 128 * g + 128], high_ref, low_ref, g)
        for r in range(8):
            c = prol_col[0, 8 * g + r]
            total[c] = total[c] + (out[16 * r : 16 * r + 8] + out[16 * r + 8 : 16 * r + 16])
    first, last = corners()
    whole = jnp.where(first | last, total[...], 0.0)
    whole = whole + other_lane(whole)
    return whole + other_row(whole)


def to_pairs(vector):
    rows = masked_rows(vector)
    n = rows.shape[0]
    lane = lax.broadcasted_iota(jnp.int32, (128, 256), 0)
    pair = lax.broadcasted_iota(jnp.int32, (128, 256), 1) // 8
    gather = ((lane % 64) == 2 * pair + lane // 64).astype(F32).astype(BF16)
    both = jnp.dot(rows.reshape(16 * n, 128), gather, preferred_element_type=F32).reshape(n, 16, 256)
    whole = both[:, :8] + both[:, 8:]
    lane8 = own_lane(256)
    return jnp.concatenate([jnp.where(lane8 == i % 8, whole[i], 0.0)[None] for i in range(n)], 0)


def pairs_kernel(vector, pairs):
    pairs[...] = to_pairs(vector[...])


def by_slot(col, i, k):
    return col[k - 1, i]


def by_row(col, i, k):
    return col[i, k - 1]


def smooth_kernel(step, count, at, col, own, outer, partner, high, low, resid, total, new_resid, new_d, new_total, window, left):
    fill_window(window, own, partner, outer)
    product = operator(functools.partial(at, col), 7, window, left, high, low, count)
    r = resid[...] - product
    d = step[0] * own[...] + step[1] * r
    new_resid[...] = r
    new_d[...] = d
    new_total[...] = total[...] + d


def total_kernel(step, count, at, col, own, outer, partner, high, low, resid, total, new_total, window, left):
    fill_window(window, own, partner, outer)
    product = operator(functools.partial(at, col), 7, window, left, high, low, count)
    new_total[...] = total[...] + step[0] * own[...] + step[1] * (resid[...] - product)


def restrict_kernel(
    count, col, prol_col, own, outer, partner, high, low, resid, back_high, back_low,
    pairs, to_partner, to_own, to_outer, window, left, sums,
):
    fill_window(window, own, partner, outer)
    product = operator_pairs(functools.partial(by_slot, col), 7, window, left, high, low, count)
    pairs[...] = product
    whole = restrict_pairs(prol_col, resid[...] - product, back_high, back_low, sums)
    m = whole.shape[0] // 3
    to_partner[...] = pack_quarters(whole[:m])
    to_own[...] = pack_quarters(whole[m : 2 * m])
    to_outer[...] = pack_quarters(whole[2 * m :])


def second_kernel(pairs, resid, second):
    second[...] = resid[...] - from_pairs(pairs[...])


def sum_kernel(own, outer, partner, total):
    total[...] = own[...] + outer[...] + partner[...]


def prolong_kernel(prol_col, own, outer, partner, high, low, total, spread, new_total, window, left):
    fill_window(window, own, partner, outer)
    product = operator(lambda i, k: prol_col[0, i], 1, window, left, high, low, None)
    spread[...] = product
    new_total[...] = total[...] + product


def resid_kernel(count, col, own, outer, partner, high, low, resid, total, new_resid, new_total, window, left):
    fill_window(window, own, partner, outer)
    product = operator(functools.partial(by_slot, col), 7, window, left, high, low, count)
    r = resid[...] - product
    new_resid[...] = r
    new_total[...] = total[...] + r


def solution_kernel(total, *rest):
    unpack_to(rest[-1], total[...])


def last_kernel(count, col, own, outer, partner, high, low, resid, *rest):
    *others, out, window, left = rest
    del others
    fill_window(window, own, outer=outer, partner=partner)
    product = operator(functools.partial(by_slot, col), 7, window, left, high, low, count)
    unpack_to(out, resid[...] - product)


def keep_solution(total, other, out):
    del total
    out[...] = other[...]


def keep_resid(*refs):
    other, out = refs[-4:-2]
    out[...] = other[...]


def operator_scratch(window_blocks, rows, slots):
    return [pltpu.VMEM((window_blocks, 16, 128), BF16), pltpu.VMEM((16 * rows, 128 * slots), BF16)]


class Chain:
    last = None

    def __init__(self, rank, parity):
        self.rank = rank
        self.parity = parity

    def call(self, kernel, name, scalars, vectors, outs, scratch, otherwise=None, ordered=True):
        def guarded(rank, previous, *refs):
            del previous

            @pl.when((rank[0] & 1) == self.parity)
            def _():
                kernel(*refs)

            if otherwise is not None:

                @pl.when((rank[0] & 1) != self.parity)
                def _():
                    otherwise(*refs)

        if Chain.last is None:
            Chain.last = vectors[0]
        results = pl.pallas_call(
            guarded,
            in_specs=[SMEM, pl.BlockSpec(memory_space=pl.ANY)] + [SMEM] * len(scalars) + [VMEM] * len(vectors),
            out_specs=[VMEM] * len(outs),
            out_shape=[
                out if isinstance(out, jax.ShapeDtypeStruct)
                else pltpu.VMEM(out if isinstance(out, tuple) else (out // 4, 8, 128), F32)
                for out in outs
            ],
            scratch_shapes=scratch,
            compiler_params=PARAMS,
            name=name,
        )(self.rank, Chain.last, *scalars, *vectors)
        if ordered:
            Chain.last = results[0]
        return results


def turns(steps):
    done = [0, 0]
    which, run = 0, 1
    while min(done) < steps:
        for _ in range(run):
            if done[which] < steps:
                yield which
                done[which] += 1
        which, run = 1 - which, 2


def packed_tiles(vector):
    q = vector.shape[0] // 4
    top = jnp.concatenate([vector[:q], vector[2 * q : 3 * q]], -1)
    bottom = jnp.concatenate([vector[3 * q :], vector[q : 2 * q]], -1)
    return jnp.concatenate([top, bottom], 1)


def pack_kernel(rank, *refs):
    del rank
    for vector, packed in zip(refs[: len(refs) // 2], refs[len(refs) // 2 :]):
        packed[...] = packed_tiles(vector)


def pack(rank, *vectors):
    blocks, sides, width = vectors[0].shape
    shape = pltpu.VMEM((blocks // 4, 2 * sides, 2 * width), F32)
    return pl.pallas_call(
        pack_kernel,
        in_specs=[SMEM] + [VMEM] * len(vectors),
        out_specs=[VMEM] * len(vectors),
        out_shape=[shape] * len(vectors),
        compiler_params=PARAMS,
        name="pack",
    )(rank, *vectors)


def unpack_to(out, packed):
    q = packed.shape[0]
    out[:q] = packed[:, :4, :64]
    out[q : 2 * q] = packed[:, 4:, 64:]
    out[2 * q : 3 * q] = packed[:, :4, 64:]
    out[3 * q :] = packed[:, 4:, :64]


def begin_kernel(n, m, slots, rank, vals, *refs):
    cols, (high_ref, low_ref), places = refs[:3], refs[3:5], refs[5:8]
    held, arrived, *small = refs[8:]
    here, there, sems = small[:3], small[3:6], small[6]
    come = [pltpu.make_async_copy(cols[i], here[i], sems.at[i]) for i in range(3)]
    leave = [pltpu.make_async_copy(there[i], places[i], sems.at[3 + i]) for i in range(3)]

    def indices():
        for i, per_device in enumerate((n, m, m)):
            come[i].wait()
            block = here[i][...]
            place = block - rank[0] * per_device
            inner = block - (rank[0] ^ 1) * per_device
            outer = lax.rem(block, per_device) + 2 * per_device
            own = (place >= 0) & (place < per_device)
            beside = (inner >= 0) & (inner < per_device)
            there[i][...] = jnp.where(own, place + per_device, jnp.where(beside, inner, outer))
            leave[i].start()

    for copy in come:
        copy.start()
    split_groups(n // 8, slots, vals, high_ref, low_ref, held, arrived, indices)
    for copy in leave:
        copy.wait()


def begin(rank, vals, m, *cols):
    n, slots, width = vals.shape
    shape = pltpu.VMEM((n // 8, 128 * slots, 256), BF16)
    hbm = pl.BlockSpec(memory_space=pltpu.HBM)
    return pl.pallas_call(
        functools.partial(begin_kernel, n, m, slots),
        in_specs=[SMEM] + [hbm] * 4,
        out_specs=[VMEM] * 2 + [SMEM] * 3,
        out_shape=[shape, shape] + [pltpu.SMEM(c.shape, jnp.int32) for c in cols],
        scratch_shapes=[
            pltpu.VMEM((n // 8, slots, 8, width), F32),
            pltpu.SemaphoreType.DMA((n // 8,)),
            *[pltpu.VMEM(c.shape, jnp.int32) for c in cols * 2],
            pltpu.SemaphoreType.DMA((6,)),
        ],
        compiler_params=STREAM_PARAMS,
        name="begin",
    )(rank, vals.transpose(1, 0, 2), *cols)


def body(right_side, fine_vals, fine_cols, prol_vals, prol_cols, coarse_vals, coarse_cols):
    devices = lax.axis_size("fine")
    rank = jnp.reshape(lax.axis_index("fine"), (1,))
    n = right_side.shape[0]
    m = coarse_vals.shape[0]

    up = [(i, (i + 1) % devices) for i in range(devices)]
    down = [((i + 1) % devices, i) for i in range(devices)]
    inside = [(i, i ^ 1) for i in range(devices)]
    across = [(i, (i + 1 if i % 2 else i - 1) % devices) for i in range(devices)]

    from_outer = lax.ppermute(right_side, "fine", across)
    from_partner = lax.ppermute(right_side, "fine", inside)
    high, low, fine_at, prol_at, coarse_at = begin(
        rank, fine_vals, m, fine_cols.T, prol_cols.reshape(1, n), coarse_cols
    )
    coarse_high, coarse_low = prepare(rank, coarse_vals)
    prol_high, prol_low, back_high, back_low = prepare_transfer(prol_vals)

    from_outer, from_partner, first = pack(rank, from_outer, from_partner, right_side)

    def steps(chain):
        def fine(kernel, name, d, more, outs, scalars=(), scratch=(), after=()):
            partner, outer = yield d, d
            vectors = (d, outer, partner, high, low, *more, *after)
            return chain.call(kernel, name, (fine_at, *scalars), vectors, outs, operator_scratch(3 * n, n, 7) + list(scratch))

        def fine_smooth(d, resid, total, step):
            kernel = functools.partial(smooth_kernel, step, n, by_slot)
            return (yield from fine(kernel, "fine_smooth", d, (resid, total), [n, n, n]))

        def fine_resid(d, resid, total):
            kernel = functools.partial(resid_kernel, n)
            return (yield from fine(kernel, "fine_resid", d, (resid, total), [n, n]))

        def coarse(kernel, name, d, resid, total, step, outs):
            partner, outer = yield d, d
            vectors = (d, outer, partner, coarse_high, coarse_low, resid, total)
            kernel = functools.partial(kernel, step, m, by_row)
            return chain.call(kernel, name, (coarse_at,), vectors, outs, operator_scratch(3 * m, m, 7))

        def cycle(resid, total):
            resid, d, total = yield from fine_smooth(resid, resid, total, STEP1)
            resid, d, total = yield from fine_smooth(d, resid, total, STEP2)
            sums = [pltpu.VMEM((3 * m, 8, 128), F32)]
            (resid_pairs,) = chain.call(pairs_kernel, "resid_pairs", (), (resid,), [(n, 8, 256)], [])
            pairs, to_partner, to_own, to_outer = yield from fine(
                functools.partial(restrict_kernel, n), "fine_restrict", d, (resid_pairs,), [(n, 8, 256), m, m, m],
                scalars=(prol_at,), scratch=sums, after=(back_high, back_low),
            )
            (second,) = chain.call(second_kernel, "fine_second", (), (pairs, resid), [n], [])
            partner, outer = yield to_partner, to_outer
            (right,) = chain.call(sum_kernel, "coarse_sum", (), (to_own, outer, partner), [m], [])
            resid, d, fix = yield from coarse(smooth_kernel, "coarse_smooth", right, right, right, STEP1, [m, m, m])
            (fix,) = yield from coarse(total_kernel, "coarse_total", d, resid, fix, STEP2, [m])
            partner, outer = yield fix, fix
            spread, total = chain.call(
                prolong_kernel, "prolong", (prol_at,),
                (fix, outer, partner, prol_high, prol_low, total), [n, n], operator_scratch(3 * m, n, 1),
            )
            resid, total = yield from fine_resid(spread, second, total)
            resid, d, total = yield from fine_smooth(resid, resid, total, STEP1)
            resid, d, total = yield from fine_smooth(d, resid, total, STEP2)
            return d, resid, total

        d, resid, total = yield from cycle(first, first)
        resid, total = yield from fine_resid(d, resid, total)
        d, resid, total = yield from cycle(resid, total)
        written[:] = chain.call(
            solution_kernel, "solution", (), (total, *written),
            [jax.ShapeDtypeStruct(right_side.shape, F32) if written else right_side.shape], [],
            keep_solution if written else None, ordered=False,
        )
        partner, outer = yield d, d
        vectors = (d, outer, partner, high, low, resid, *finished)
        finished[:] = chain.call(
            functools.partial(last_kernel, n), "fine_last", (fine_at,), vectors,
            [jax.ShapeDtypeStruct(right_side.shape, F32)], operator_scratch(3 * n, n, 7), keep_resid if finished else None,
        )

    written, finished = [], []
    Chain.last = None
    chains = [steps(Chain(rank, 1)), steps(Chain(rank, 0))]
    for chain in chains:
        next(chain)
    inbox = [[(from_partner, from_outer)], [(from_partner, from_outer)]]
    for which in turns(22):
        try:
            to_partner, to_outer = chains[which].send(inbox[which].pop(0))
        except StopIteration:
            continue
        partner = lax.ppermute(to_partner, "fine", inside)
        outer = lax.ppermute(to_outer, "fine", (up, down)[which])
        inbox[1 - which].append((partner, outer))
    return written[0], finished[0]


def solution(mesh):
    in_specs = (
        P("fine", None, None),
        P("fine", None, None),
        P("fine", None),
        P("fine", None),
        P("fine"),
        P("fine", None, None),
        P("fine", None),
    )
    out_specs = (P("fine", None, None), P("fine", None, None))
    return jax.shard_map(body, mesh=mesh, in_specs=in_specs, out_specs=out_specs, check_vma=False)
```
